32 devices in a mesh: vol: 16 (over z, y, x), path: 2 (over core).
Axes of the slice: x: 2, y: 2, z: 4, core: 2. Of those that a mesh axis runs over, the one named last changes fastest.
Arguments:
- factors: bfloat16 [16, 2048], P(None, 'path'), may hold values from -6 to 6
- payoff: float32 [4, 2048], P(None, 'path'), may hold values from -6 to 6
- terminal: float32 [16, 2048], P('vol', 'path'), may hold values from 0.5 to 4
- decisions: int32 [3, 16, 2048], P(None, 'vol', 'path'), may hold values 0 or 1
- level_range: int32 [4, 2], replicated, may hold values from 1 to 15, as said below
- w_in_master: float32 [16, 16, 1024], P('vol'), may hold values from -1.5 to 1.5
- w_mid_master: float32 [16, 1024, 1024], P('vol', 'path'), may hold values from -0.1875 to 0.1875
- vec_master: float32 [16, 3, 1024], P('vol'), may hold values from -0.6 to 0.6
- w_in_copy: bfloat16 [16, 16, 1024], P('vol'), may hold values from -1.5 to 1.5
- w_mid_copy: bfloat16 [16, 1024, 1024], P('vol', 'path'), may hold values from -0.1875 to 0.1875
- mom_in: float32 [16, 16, 1024], P('vol'), may hold values from -0.6 to 0.6
- mom_mid: float32 [16, 1024, 1024], P('vol', 'path'), may hold values from -0.6 to 0.6
- mom_vec: float32 [16, 3, 1024], P('vol'), may hold values from -0.6 to 0.6
Outputs:
- level_value: float32 [16], P('vol')
- new_w_in: float32 [16, 16, 1024], P('vol')
- new_w_mid: float32 [16, 1024, 1024], P('vol', 'path')
- new_vec: float32 [16, 3, 1024], P('vol')
- new_mom_in: float32 [16, 16, 1024], P('vol')
- new_mom_mid: float32 [16, 1024, 1024], P('vol', 'path')
- new_mom_vec: float32 [16, 3, 1024], P('vol')
- new_in_copy: bfloat16 [16, 16, 1024], P('vol')
- new_mid_copy: bfloat16 [16, 1024, 1024], P('vol', 'path')
The draws below stay inside these ranges and needn't reach their ends.
Inputs may be any that keep to these rules, and one draw needn't show every extreme that they name: At every date level_range[s, 0] <= level_range[s, 1] and level 0 lies below the range; at dates 1 to 3 the range starts at level 1; at date 0 the range holds exactly 8 levels.
All inputs are finite; a program needn't handle non-finite values. No bound on the sum of `decisions` on one device may be relied on, other than what follows from the above.
Results may differ from the reference program's by a relative error of at most 0.015.
Values may be sent and summed in bfloat16 or wider, within the bound.
No kernel may reach another device: no remote copies, remote signals or barrier semaphores. Data moves between devices by JAX's collectives and lax.ppermute only.
A program may use at most 64 MiB of HBM per device.

```python
import math
import jax
import jax.numpy as jnp
from jax import lax

FACTORS = 16
HIDDEN_SIZE = 1024
DATES = 4
LEVELS = 16
PATHS = 2048


def draw_level_range(key, part):
    key_upper, key_start = jax.random.split(key, 2)
    lower_end = jnp.ones((DATES,), jnp.int32)
    upper_end = jax.random.randint(key_upper, (DATES,), LEVELS // 2, LEVELS)
    start_low = jax.random.randint(key_start, (), 1, LEVELS // 2 + 1)
    lower_end = lower_end.at[0].set(start_low)
    upper_end = upper_end.at[0].set(start_low + LEVELS // 2 - 1)
    return jnp.stack([lower_end, upper_end], axis=1).astype(jnp.int32)


def place_ends(entries, key, least, high):
    dims = entries.shape
    place = [jax.random.randint(jax.random.fold_in(key, axis), (), 0, dims[axis]) for axis in range(len(dims))]
    entries = entries.at[tuple(place)].set(least)
    longest = dims.index(max(dims))
    place[longest] = (place[longest] + 1) % dims[longest]
    return entries.at[tuple(place)].set(high)


def block_levels(rng, dims, cuts, least, high):
    def one(position, blocks):
        heights = jax.random.uniform(jax.random.fold_in(jax.random.fold_in(rng, 6), position), (blocks,), jnp.float32, least / len(cuts), high / len(cuts))
        return jnp.repeat(jnp.exp(heights), dims[position] // blocks).reshape((-1,) + (1,) * (len(dims) - position - 1))

    factor_of = one(*cuts[0])
    for cut in cuts[1:]:
        factor_of = factor_of * one(*cut)
    return factor_of


def noise(own_key, shape, scale, limit, shards=(), kind=jnp.bfloat16):
    values = jax.random.normal(own_key, shape, jnp.float32) * scale
    if len(shards) > 0:
        values = block_levels(own_key, shape, shards, -0.22, 0.18) * values
    return jnp.clip(values, min=-limit, max=limit).astype(kind)


def setup_inputs(seed: int = 0) -> dict:
    seeds = jax.random.split(jax.random.key(seed), 14)
    factors = noise(seeds[0], (FACTORS, PATHS), 1.0, 6.0, ((1, 2),))
    payoff = noise(seeds[1], (DATES, PATHS), 1.0, 6.0, ((1, 2),), jnp.float32)
    terminal = jnp.clip(jnp.exp(math.log(4.0) - 2.0794415 * jax.random.uniform(seeds[2], (LEVELS, PATHS), jnp.float32) ** block_levels(seeds[2], (LEVELS, PATHS), ((0, 16), (1, 2)), -0.2, 0.2)), 0.5, 4.0)
    decisions = place_ends((jax.random.randint(seeds[3], (DATES - 1, LEVELS, PATHS), 0, 2) < 1).astype(jnp.int32), jax.random.fold_in(seeds[3], 1), 0, 1)
    level_range = draw_level_range(jax.random.fold_in(seeds[13], 71), 0)
    w_in_master = noise(seeds[5], (LEVELS, FACTORS, HIDDEN_SIZE), FACTORS ** -0.5, 1.5, ((0, 16),), jnp.float32)
    w_mid_master = noise(seeds[6], (LEVELS, HIDDEN_SIZE, HIDDEN_SIZE), HIDDEN_SIZE ** -0.5, 0.1875, ((0, 16), (1, 2)), jnp.float32)
    vec_master = noise(seeds[7], (LEVELS, 3, HIDDEN_SIZE), 0.1, 0.6, ((0, 16),), jnp.float32)
    w_in_copy = noise(seeds[8], (LEVELS, FACTORS, HIDDEN_SIZE), FACTORS ** -0.5, 1.5, ((0, 16),))
    w_mid_copy = noise(seeds[9], (LEVELS, HIDDEN_SIZE, HIDDEN_SIZE), HIDDEN_SIZE ** -0.5, 0.1875, ((0, 16), (1, 2)))
    mom_in = noise(seeds[10], (LEVELS, FACTORS, HIDDEN_SIZE), 0.1, 0.6, ((0, 16),), jnp.float32)
    mom_mid = noise(seeds[11], (LEVELS, HIDDEN_SIZE, HIDDEN_SIZE), 0.1, 0.6, ((0, 16), (1, 2)), jnp.float32)
    mom_vec = noise(seeds[12], (LEVELS, 3, HIDDEN_SIZE), 0.1, 0.6, ((0, 16),), jnp.float32)
    return {"factors": factors, "payoff": payoff, "terminal": terminal, "decisions": decisions, "level_range": level_range, "w_in_master": w_in_master, "w_mid_master": w_mid_master, "vec_master": vec_master, "w_in_copy": w_in_copy, "w_mid_copy": w_mid_copy, "mom_in": mom_in, "mom_mid": mom_mid, "mom_vec": mom_vec}


MOMENTUM = 0.9
STEP_SIZE = 0.01


def silu_parts(preact):
    squash = jax.nn.sigmoid(preact)
    return preact * squash, squash * (1.0 + preact * (1.0 - squash))


def level_pass(w_first, w_second, vectors, features, gain_row):
    pre_one = lax.dot_general(features, w_first, (((0,), (0,)), ((), ())), preferred_element_type=jnp.float32) + vectors[0]
    act_one, slope_one = silu_parts(pre_one)
    hidden_one = act_one.astype(jnp.bfloat16)
    pre_two = jnp.dot(hidden_one, w_second, preferred_element_type=jnp.float32) + vectors[1]
    act_two, slope_two = silu_parts(pre_two)
    hidden_two = act_two.astype(jnp.bfloat16)
    logits = jnp.sum(hidden_two.astype(jnp.float32) * vectors[2], axis=1)
    chance = jax.nn.sigmoid(logits)
    d_logit = -gain_row * chance * (1.0 - chance)
    d_head = jnp.sum(d_logit[:, None] * hidden_two.astype(jnp.float32), axis=0)
    d_pre_two = d_logit[:, None] * vectors[2] * slope_two
    d_bias_two = jnp.sum(d_pre_two, axis=0)
    d_two_low = d_pre_two.astype(jnp.bfloat16)
    d_second = lax.dot_general(hidden_one, d_two_low, (((0,), (0,)), ((), ())), preferred_element_type=jnp.float32)
    d_hidden_one = lax.dot_general(d_two_low, w_second, (((1,), (1,)), ((), ())), preferred_element_type=jnp.float32)
    d_pre_one = d_hidden_one * slope_one
    d_bias_one = jnp.sum(d_pre_one, axis=0)
    d_first = jnp.dot(features, d_pre_one.astype(jnp.bfloat16), preferred_element_type=jnp.float32)
    d_vectors = jnp.stack([d_bias_one, d_bias_two, d_head])
    return d_first, d_second, d_vectors, jnp.sum(chance * gain_row)


def reference(factors, payoff, terminal, decisions, level_range, w_in_master, w_mid_master, vec_master, w_in_copy, w_mid_copy, mom_in, mom_mid, mom_vec):
    levels = jnp.arange(LEVELS, dtype=jnp.int32)[:, None]
    zero_row = jnp.zeros((1, PATHS), jnp.float32)
    carry_value = terminal
    for date_index in range(DATES - 1, 0, -1):
        lower_row = jnp.concatenate([zero_row, carry_value[:-1]], axis=0)
        lower_end = level_range[date_index, 0]
        upper_end = level_range[date_index, 1]
        inside = jnp.logical_and(levels >= lower_end, levels <= upper_end)
        taken_now = jnp.where(levels > upper_end, 1.0, jnp.where(inside, decisions[date_index - 1].astype(jnp.float32), 0.0))
        carry_value = taken_now * (payoff[date_index] + lower_row) + (1.0 - taken_now) * carry_value
    lower_row = jnp.concatenate([zero_row, carry_value[:-1]], axis=0)
    gain_all = payoff[0] + lower_row - carry_value
    low_now = level_range[0, 0]
    high_now = level_range[0, 1]
    active_span = LEVELS // 2

    def select_active(array):
        return lax.dynamic_slice_in_dim(array, low_now, active_span, 0)

    def one_level(level_items):
        return level_pass(level_items[0], level_items[1], level_items[2], factors, level_items[3])

    d_first, d_second, d_vectors, value_sums = lax.map(one_level, (select_active(w_in_copy), select_active(w_mid_copy), select_active(vec_master), select_active(gain_all)))

    def put_back(block, shape):
        return lax.dynamic_update_slice_in_dim(jnp.zeros(shape, jnp.float32), block, low_now, 0)

    grad_in = put_back(d_first, w_in_master.shape)
    grad_mid = put_back(d_second, w_mid_master.shape)
    grad_vec = put_back(d_vectors, vec_master.shape)
    value_active = put_back(value_sums, (LEVELS,))
    level_ids = levels[:, 0]
    active = jnp.logical_and(level_ids >= low_now, level_ids <= high_now)
    forced = jnp.where(level_ids > high_now, 1.0, 0.0)
    value_total = jnp.where(active, value_active, forced * jnp.sum(gain_all, axis=1)) + jnp.sum(carry_value, axis=1)
    level_value = value_total / PATHS
    new_mom_in = MOMENTUM * mom_in + grad_in
    new_mom_mid = MOMENTUM * mom_mid + grad_mid
    new_mom_vec = MOMENTUM * mom_vec + grad_vec
    new_w_in = w_in_master - STEP_SIZE * new_mom_in
    new_w_mid = w_mid_master - STEP_SIZE * new_mom_mid
    new_vec = vec_master - STEP_SIZE * new_mom_vec
    return (level_value, new_w_in, new_w_mid, new_vec, new_mom_in, new_mom_mid, new_mom_vec, new_w_in.astype(jnp.bfloat16), new_w_mid.astype(jnp.bfloat16))
```

```python
import jax
import jax.numpy as jnp
from jax import lax
from jax.experimental import pallas as pl
from jax.experimental.pallas import tpu as pltpu
from jax.sharding import PartitionSpec as P

MOMENTUM = 0.9
STEP_SIZE = 0.01
LOWER_LEVELS = 4
SMALL_ROWS = 24
VMEM_LIMIT = 30 * 1024 * 1024


def vmem_specs(count):
    return [pl.BlockSpec(memory_space=pltpu.VMEM)] * count


def call(kernel, out_shape, in_specs, name, flops, scratch=(), **options):
    return pl.pallas_call(
        kernel,
        out_shape=out_shape,
        in_specs=in_specs,
        out_specs=jax.tree.map(lambda _: pl.BlockSpec(memory_space=pltpu.VMEM), out_shape),
        scratch_shapes=list(scratch),
        compiler_params=pltpu.CompilerParams(vmem_limit_bytes=VMEM_LIMIT, **options),
        cost_estimate=pl.CostEstimate(flops=flops, bytes_accessed=1 << 20, transcendentals=0),
        name=name,
    )


def half_columns(flip, half, width):
    return pl.ds(pl.multiple_of((flip ^ half) * width, width), width)


def silu_parts(preact):
    squash = 0.5 + 0.5 * jnp.tanh(0.5 * preact)
    act = preact * squash
    return act, squash + act * (1.0 - squash)


def first_layer(flip_of, factors, w_in, vectors, hidden_one, slope_one):
    flip = flip_of()
    hidden = w_in.shape[1]
    width, paths, tile, rows = hidden // 2, factors.shape[1], 128, 32
    for half in range(2):
        columns = half_columns(flip, half, width)
        weights = w_in[:, columns]
        bias = vectors[0, :, columns]
        place = slice(half * width, (half + 1) * width)
        for start in range(0, paths, tile):
            pre = lax.dot_general(
                factors[:, start : start + tile],
                weights,
                (((0,), (0,)), ((), ())),
                preferred_element_type=jnp.float32,
            )
            for row in range(0, tile, rows):
                act, slope = silu_parts(pre[row : row + rows] + bias)
                here = slice(start + row, start + row + rows)
                hidden_one[here, place] = act.astype(jnp.bfloat16)
                slope_one[here, place] = slope.astype(jnp.bfloat16)


def continuation(level, level_range, payoff, row_sets):
    dates = payoff.shape[0]
    conts = [
        jnp.where(level >= below, rows[0:1, :], 0.0) for below, rows in enumerate(row_sets)
    ]
    for date in range(dates - 1, 0, -1):
        low, high = level_range[0, date], level_range[1, date]
        updated = []
        for below in range(len(conts) - 1):
            here = level - below
            chosen = row_sets[below][dates - date : dates - date + 1, :]
            inside = jnp.logical_and(here >= low, here <= high)
            taken = jnp.where(here > high, 1.0, jnp.where(inside, chosen, 0.0))
            value = taken * (payoff[date : date + 1, :] + conts[below + 1]) + (1.0 - taken) * conts[below]
            updated.append(jnp.where(here >= 0, value, 0.0))
        conts = updated
    return conts


def second_layer(
    hidden_one, w_own, w_other, vectors, level_range, payoff, own, low1, low2, low3, low4,
    d_two, grad_other, sums, gain_column, weighted_slope, act_two,
):
    level = lax.axis_index("vol")
    paths, hidden = hidden_one.shape
    width, tile, rows = hidden // 2, 128, 16
    row_sets = [ref[...] for ref in (own, low1, low2, low3, low4)]
    cont_here, cont_below = continuation(level, level_range, payoff, row_sets)
    gain = payoff[0:1, :] + cont_below - cont_here
    gain_column[...] = jnp.transpose(jnp.broadcast_to(gain, (8, paths)))
    low_now, high_now = level_range[0, 0], level_range[1, 0]
    active = jnp.logical_and(level >= low_now, level <= high_now)
    enabled = jnp.where(active, 1.0, 0.0)
    forced = jnp.where(level > high_now, 1.0, 0.0)
    bias, head = vectors[1], vectors[2]
    bias_sum = jnp.zeros((8, hidden), jnp.float32)
    head_sum = jnp.zeros((8, hidden), jnp.float32)
    value_sum = jnp.zeros((rows, 1), jnp.float32)
    for index, start in enumerate(range(0, paths, tile)):
        here = slice(start, start + tile)
        slot = index % 2
        pre = jnp.dot(hidden_one[here, :width], w_own[...], preferred_element_type=jnp.float32)
        pre += jnp.dot(hidden_one[here, width:], w_other[...], preferred_element_type=jnp.float32)
        d_logits = []
        for row in range(0, tile, rows):
            act, slope = silu_parts(pre[row : row + rows] + bias)
            act = act.astype(jnp.bfloat16).astype(jnp.float32)
            weighted_slope[slot, row : row + rows, :] = slope * head
            act_two[slot, row : row + rows, :] = act
            logits = jnp.sum(act * head, axis=1, keepdims=True)
            chance = 0.5 + 0.5 * jnp.tanh(0.5 * logits)
            gains = gain_column[start + row : start + row + rows, 0:1]
            d_logits.append(-enabled * gains * chance * (1.0 - chance))
            value_sum += chance * gains
        for row in range(0, tile, rows):
            d_logit = d_logits[row // rows]
            d_pre = d_logit * weighted_slope[slot, row : row + rows, :]
            scaled = d_logit * act_two[slot, row : row + rows, :]
            d_two[start + row : start + row + rows, :] = d_pre.astype(jnp.bfloat16)
            for part in range(0, rows, 8):
                bias_sum += d_pre[part : part + 8]
                head_sum += scaled[part : part + 8]
    chunk = 256
    for column in range(0, hidden, chunk):
        place = slice(column, column + chunk)
        grad_other[:, place] = lax.dot_general(
            hidden_one[:, width:],
            d_two[:, place],
            (((0,), (0,)), ((), ())),
            preferred_element_type=jnp.float32,
        ).astype(jnp.bfloat16)
    value_total = enabled * jnp.sum(value_sum) + forced * jnp.sum(gain) + jnp.sum(cont_here)
    sums[0:1, :] = jnp.sum(bias_sum, axis=0, keepdims=True)
    sums[1:2, :] = jnp.sum(head_sum, axis=0, keepdims=True)
    sums[2:3, :] = jnp.full((1, hidden), value_total, jnp.float32)
    sums[3:8, :] = jnp.zeros((5, hidden), jnp.float32)


def backward(flip_of, hidden_one, d_two, w_own, w_other, slope_one, factors, sums, grad_own, small, d_one):
    flip = flip_of()
    paths, hidden = hidden_one.shape
    width, tile, rows = hidden // 2, 128, 32
    count = factors.shape[0]
    bias_sums = [jnp.zeros((8, width), jnp.float32) for _ in range(2)]
    for start in range(0, paths, tile):
        for half, weights in enumerate((w_own, w_other)):
            place = slice(half * width, (half + 1) * width)
            d_hidden = lax.dot_general(
                d_two[start : start + tile, :],
                weights[...],
                (((1,), (1,)), ((), ())),
                preferred_element_type=jnp.float32,
            )
            for row in range(0, tile, rows):
                here = slice(start + row, start + row + rows)
                d_pre = d_hidden[row : row + rows] * slope_one[here, place].astype(jnp.float32)
                d_one[here, place] = d_pre.astype(jnp.bfloat16)
                for part in range(0, rows, 8):
                    bias_sums[half] += d_pre[part : part + 8]
    for half in range(2):
        columns = half_columns(flip, half, width)
        place = slice(half * width, (half + 1) * width)
        small[0:count, columns] = jnp.dot(
            factors[...], d_one[:, place], preferred_element_type=jnp.float32
        )
        small[count : count + 1, columns] = jnp.sum(bias_sums[half], axis=0, keepdims=True)
    small[count + 1 : count + 4, :] = sums[0:3, :]
    small[count + 4 : SMALL_ROWS, :] = jnp.zeros((SMALL_ROWS - count - 4, hidden), jnp.float32)
    chunk = 256
    for column in range(0, hidden, chunk):
        place = slice(column, column + chunk)
        grad_own[:, place] = lax.dot_general(
            hidden_one[:, :width],
            d_two[:, place],
            (((0,), (0,)), ((), ())),
            preferred_element_type=jnp.float32,
        )


def update(
    paths_total, grad_own, grad_other, small_own, small_other, mom_mid, w_mid, mom_in, w_in, mom_vec, vec,
    value, new_w_in, new_w_mid, new_vec, new_mom_in, new_mom_mid, new_mom_vec, new_in_copy, new_mid_copy,
):
    mom = MOMENTUM * mom_mid[...] + (grad_own[...] + grad_other[...].astype(jnp.float32))
    new_mom_mid[...] = mom
    master = w_mid[...] - STEP_SIZE * mom
    new_w_mid[...] = master
    new_mid_copy[...] = master.astype(jnp.bfloat16)

    @pl.when(pl.program_id(0) == 0)
    def _():
        small = small_own[...] + small_other[...]
        count = mom_in.shape[0]
        mom_first = MOMENTUM * mom_in[...] + small[:count]
        new_mom_in[...] = mom_first
        first = w_in[...] - STEP_SIZE * mom_first
        new_w_in[...] = first
        new_in_copy[...] = first.astype(jnp.bfloat16)
        for row in range(3):
            mom_row = MOMENTUM * mom_vec[row] + small[count + row : count + row + 1]
            new_mom_vec[row] = mom_row
            new_vec[row] = vec[row] - STEP_SIZE * mom_row
        value[0] = small[count + 3, 0] / paths_total


def step_of(mesh):
    levels, cores = mesh.shape["vol"], mesh.shape["path"]
    paired = cores == 2

    def flip_of():
        return lax.axis_index("path") if paired else 0

    def swap(value):
        return lax.ppermute(value, "path", [(0, 1), (1, 0)])

    def shards(
        factors, payoff, terminal, decisions, level_range, w_in_master, w_mid_master, vec_master,
        w_in_copy, w_mid_copy, mom_in, mom_mid, mom_vec,
    ):
        paths = factors.shape[1]
        count, hidden = w_in_copy.shape[1:]
        width = hidden // 2
        f32, bf16 = jnp.float32, jnp.bfloat16
        vectors = vec_master.transpose(1, 0, 2)
        if paired:
            w_own = w_mid_copy[0]
            w_other = swap(w_own)
        else:
            w_full = lax.all_gather(w_mid_copy[0], "path", axis=0, tiled=True)
            w_own, w_other = w_full[:width], w_full[width:]
        dates = payoff.shape[0]
        rows = jnp.concatenate(
            [terminal] + [decisions[date - 1].astype(f32) for date in range(dates - 1, 0, -1)]
        )
        lower = [
            lax.ppermute(rows, "vol", [(here, (here + below) % levels) for here in range(levels)])
            for below in range(1, LOWER_LEVELS + 1)
        ]
        square = 2 * paths * hidden * hidden
        hidden_one, slope_one = call(
            lambda *refs: first_layer(flip_of, *refs),
            (jax.ShapeDtypeStruct((paths, hidden), bf16),) * 2,
            vmem_specs(3),
            "first_layer",
            square,
        )(factors, w_in_copy[0], vectors)
        ranges = level_range.T
        d_two, grad_other, sums = call(
            second_layer,
            (
                jax.ShapeDtypeStruct((paths, hidden), bf16),
                jax.ShapeDtypeStruct((width, hidden), bf16),
                jax.ShapeDtypeStruct((8, hidden), f32),
            ),
            vmem_specs(4) + [pl.BlockSpec(memory_space=pltpu.SMEM)] + vmem_specs(6),
            "second_layer",
            2 * square,
            scratch=(
                pltpu.VMEM((paths, 8), f32),
                pltpu.VMEM((2, 128, hidden), f32),
                pltpu.VMEM((2, 128, hidden), f32),
            ),
        )(hidden_one, w_own, w_other, vectors, ranges, payoff, rows, *lower)
        if paired:
            grad_other = swap(grad_other)
        grad_own, small = call(
            lambda *refs: backward(flip_of, *refs),
            (
                jax.ShapeDtypeStruct((width, hidden), f32),
                jax.ShapeDtypeStruct((SMALL_ROWS, hidden), f32),
            ),
            vmem_specs(7),
            "backward",
            2 * square,
            scratch=(pltpu.VMEM((paths, hidden), bf16),),
        )(hidden_one, d_two, w_own, w_other, slope_one, factors, sums)
        if paired:
            small_other = swap(small)
        else:
            grads = jnp.concatenate([grad_own.astype(bf16), grad_other])
            grad_own = lax.psum_scatter(grads, "path", scatter_dimension=0, tiled=True).astype(f32)
            grad_other = jnp.zeros(grad_own.shape, bf16)
            small = lax.psum(small, "path")
            small_other = jnp.zeros_like(small)
        own_rows = w_mid_copy.shape[1]
        block = min(64, own_rows)
        mid_block = pl.BlockSpec((block, hidden), lambda i: (i, 0))
        whole = lambda *shape: pl.BlockSpec(shape, lambda i: (0,) * len(shape))
        in_block, vec_block = whole(count, hidden), whole(3, 1, hidden)
        outs = pl.pallas_call(
            lambda *refs: update(paths * cores, *refs),
            grid=(own_rows // block,),
            in_specs=[
                mid_block, mid_block, whole(SMALL_ROWS, hidden), whole(SMALL_ROWS, hidden),
                mid_block, mid_block, in_block, in_block, vec_block, vec_block,
            ],
            out_specs=[
                pl.BlockSpec(memory_space=pltpu.SMEM),
                in_block, mid_block, vec_block, in_block, mid_block, vec_block, in_block, mid_block,
            ],
            out_shape=[
                jax.ShapeDtypeStruct((1,), f32),
                jax.ShapeDtypeStruct((count, hidden), f32),
                jax.ShapeDtypeStruct((own_rows, hidden), f32),
                jax.ShapeDtypeStruct((3, 1, hidden), f32),
                jax.ShapeDtypeStruct((count, hidden), f32),
                jax.ShapeDtypeStruct((own_rows, hidden), f32),
                jax.ShapeDtypeStruct((3, 1, hidden), f32),
                jax.ShapeDtypeStruct((count, hidden), bf16),
                jax.ShapeDtypeStruct((own_rows, hidden), bf16),
            ],
            compiler_params=pltpu.CompilerParams(vmem_limit_bytes=VMEM_LIMIT),
            cost_estimate=pl.CostEstimate(flops=0, bytes_accessed=10 << 20, transcendentals=0),
            name="update",
        )(
            grad_own, grad_other, small, small_other, mom_mid[0], w_mid_master[0],
            mom_in[0], w_in_master[0], mom_vec.transpose(1, 0, 2), vectors,
        )
        value, new_w_in, new_w_mid, new_vec, new_mom_in, new_mom_mid, new_mom_vec, in_copy, mid_copy = outs
        return (
            value,
            new_w_in[None],
            new_w_mid[None],
            new_vec.transpose(1, 0, 2),
            new_mom_in[None],
            new_mom_mid[None],
            new_mom_vec.transpose(1, 0, 2),
            in_copy[None],
            mid_copy[None],
        )

    return shards


def solution(mesh):
    vectors = P("vol", None, None)
    middle = P("vol", "path", None)
    in_specs = (
        P(None, "path"),
        P(None, "path"),
        P("vol", "path"),
        P(None, "vol", "path"),
        P(),
        vectors,
        middle,
        vectors,
        vectors,
        middle,
        vectors,
        middle,
        vectors,
    )
    out_specs = (P("vol"), vectors, middle, vectors, vectors, middle, vectors, vectors, middle)
    return jax.shard_map(step_of(mesh), mesh=mesh, in_specs=in_specs, out_specs=out_specs, check_vma=False)
```

```python
import jax
import jax.numpy as jnp
from jax import lax
from jax.experimental import pallas as pl
from jax.experimental.pallas import tpu as pltpu
from jax.sharding import PartitionSpec as P

MOMENTUM = 0.9
STEP_SIZE = 0.01
LOWER_LEVELS = 4
SMALL_ROWS = 24
LANES = 128
VMEM_LIMIT = 30 * 1024 * 1024
F32, BF16 = jnp.float32, jnp.bfloat16
VMEM_SPEC = pl.BlockSpec(memory_space=pltpu.VMEM)
HBM_SPEC = pl.BlockSpec(memory_space=pltpu.HBM)


def far(value):
    return pltpu.with_memory_space_constraint(value, pltpu.HBM)


def shape(*dims, dtype=F32):
    return jax.ShapeDtypeStruct(dims, dtype)


def call(kernel, out_shape, in_specs, name, flops, out_specs=None, scratch=()):
    return pl.pallas_call(
        kernel,
        out_shape=out_shape,
        in_specs=in_specs,
        out_specs=out_specs or [VMEM_SPEC] * len(out_shape),
        scratch_shapes=list(scratch),
        compiler_params=pltpu.CompilerParams(vmem_limit_bytes=VMEM_LIMIT),
        cost_estimate=pl.CostEstimate(flops=flops, bytes_accessed=1 << 20, transcendentals=0),
        name=name,
    )


def half_columns(flip, half, width):
    return pl.ds(pl.multiple_of((flip ^ half) * width, width), width)


def is_active(flags):
    return flags[0, 0] > 0.5


def prepare(
    terminal, decisions, ranges, payoff, factors, w_in, vectors,
    rows, flags, payoff_out, factors_out, w_in_out, vectors_out,
    terminal_here, decisions_here, ranges_here, sems,
):
    copies = [
        pltpu.make_async_copy(source, target, sems.at[index])
        for index, (source, target) in enumerate(
            (
                (ranges, ranges_here),
                (terminal, terminal_here),
                (decisions, decisions_here),
                (payoff, payoff_out),
                (factors, factors_out),
                (w_in, w_in_out),
                (vectors, vectors_out),
            )
        )
    ]
    for copy in copies:
        copy.start()
    for copy in copies:
        copy.wait()
    level = lax.axis_index("vol")
    dates = payoff.shape[0]
    rows[0:1, :] = terminal_here[...]
    for date in range(dates - 1, 0, -1):
        low, high = ranges_here[0, date], ranges_here[1, date]
        inside = jnp.logical_and(level >= low, level <= high)
        chosen = decisions_here[date - 1].astype(F32)
        taken = jnp.where(level > high, 1.0, jnp.where(inside, chosen, 0.0))
        rows[dates - date : dates - date + 1, :] = taken
    low, high = ranges_here[0, 0], ranges_here[1, 0]
    active = jnp.logical_and(level >= low, level <= high)
    flags[0:8, :] = jnp.full((8, LANES), jnp.where(active, 1.0, 0.0))
    flags[8:16, :] = jnp.full((8, LANES), jnp.where(level > high, 1.0, 0.0))


def silu_parts(preact):
    half = 0.5 * preact
    bent = jnp.tanh(half)
    upper = 1.0 + bent
    act = half * upper
    return act, upper + act * (1.0 - bent)


def first_layer(flip_of, flags, factors, w_in, vectors, hidden_one, slope_one):
    @pl.when(is_active(flags))
    def _():
        flip = flip_of()
        hidden = w_in.shape[1]
        width, paths, tile, rows = hidden // 2, factors.shape[1], 256, 16
        for half in range(2):
            columns = half_columns(flip, half, width)
            weights = w_in[:, columns]
            bias = vectors[0, :, columns]
            place = slice(half * width, (half + 1) * width)
            for start in range(0, paths, tile):
                pre = lax.dot_general(
                    factors[:, start : start + tile],
                    weights,
                    (((0,), (0,)), ((), ())),
                    preferred_element_type=F32,
                )
                for row in range(0, tile, rows):
                    act, slope = silu_parts(pre[row : row + rows] + bias)
                    here = slice(start + row, start + row + rows)
                    hidden_one[here, place] = act.astype(BF16)
                    slope_one[here, place] = (0.5 * slope).astype(BF16)


def continuation(level, payoff, row_sets):
    dates = payoff.shape[0]
    conts = [jnp.where(level >= below, rows[0:1, :], 0.0) for below, rows in enumerate(row_sets)]
    for date in range(dates - 1, 0, -1):
        updated = []
        for below in range(len(conts) - 1):
            taken = row_sets[below][dates - date : dates - date + 1, :]
            value = taken * (payoff[date : date + 1, :] + conts[below + 1]) + (1.0 - taken) * conts[below]
            updated.append(jnp.where(level >= below, value, 0.0))
        conts = updated
    return conts


def second_layer(
    flags, hidden_one, w_own, w_other, vectors, payoff, own, low1, low2, low3, low4,
    d_two, grad_other, sums, gains, pre, weighted, act_two, parts,
):
    level = lax.axis_index("vol")
    paths, hidden = hidden_one.shape
    width, tile, rows, chunks = hidden // 2, 256, 16, 4
    lane_tiles = hidden // LANES
    row_sets = [ref[...] for ref in (own, low1, low2, low3, low4)]
    cont_here, cont_below = continuation(level, payoff, row_sets)
    gain = payoff[0:1, :] + cont_below - cont_here
    base_value = flags[8, 0] * jnp.sum(gain) + jnp.sum(cont_here)

    @pl.when(jnp.logical_not(is_active(flags)))
    def _():
        grad_other[...] = jnp.zeros(grad_other.shape, BF16)
        sums[...] = jnp.zeros(sums.shape, F32)
        sums[2:3, :] = jnp.full((1, hidden), base_value, F32)

    @pl.when(is_active(flags))
    def _():
        gains[...] = jnp.transpose(jnp.broadcast_to(gain, (LANES, paths)))
        bias, head = vectors[1], vectors[2]
        half_head = 0.5 * head
        ones = jnp.ones((2 * LANES, LANES), BF16)
        bias_sums = [jnp.zeros((8, LANES), F32) for _ in range(lane_tiles)]
        head_sums = [jnp.zeros((8, LANES), F32) for _ in range(lane_tiles)]
        value_sum = jnp.zeros((rows, LANES), F32)

        def product(start, columns):
            here = slice(start, start + tile)
            return jnp.dot(
                hidden_one[here, :width], w_own[:, columns], preferred_element_type=F32
            ) + jnp.dot(hidden_one[here, width:], w_other[:, columns], preferred_element_type=F32)

        count = paths // tile
        for step in range(count + 1):
            slot, last = step % 2, (step - 1) % 2
            for chunk in range(chunks):
                if step < count:
                    columns = slice(chunk * hidden // chunks, (chunk + 1) * hidden // chunks)
                    pre[slot, :, columns] = product(step * tile, columns)
                if step > 0:
                    for row in range(chunk * tile // chunks, (chunk + 1) * tile // chunks, rows):
                        here = slice(row, row + rows)
                        act, slope = silu_parts(pre[last, here, :] + bias)
                        weighted[last, here, :] = slope * half_head
                        act_two[last, here, :] = act
                        terms = act * head
                        part = terms[:, :LANES]
                        for lane in range(1, lane_tiles):
                            part += terms[:, lane * LANES : (lane + 1) * LANES]
                        upper = part.astype(BF16)
                        parts[last, here, :LANES] = upper
                        parts[last, here, LANES:] = (part - upper.astype(F32)).astype(BF16)
            if step > 0:
                start = (step - 1) * tile
                logits = jnp.dot(parts[last], ones, preferred_element_type=F32)
                for row in range(0, tile, rows):
                    here = slice(row, row + rows)
                    there = slice(start + row, start + row + rows)
                    chance = 0.5 + 0.5 * jnp.tanh(0.5 * logits[here])
                    weight = gains[there, :] * chance
                    value_sum += weight
                    d_logit = weight * (chance - 1.0)
                    for lane in range(lane_tiles):
                        place = slice(lane * LANES, (lane + 1) * LANES)
                        d_pre = d_logit * weighted[last, here, place]
                        scaled = d_logit * act_two[last, here, place]
                        d_two[there, place] = d_pre.astype(BF16)
                        for part in range(0, rows, 8):
                            bias_sums[lane] += d_pre[part : part + 8]
                            head_sums[lane] += scaled[part : part + 8]
        grad_other[...] = lax.dot_general(
            hidden_one[:, width:], d_two[...], (((0,), (0,)), ((), ())), preferred_element_type=F32
        ).astype(BF16)
        value_total = base_value + jnp.sum(value_sum) / LANES
        for lane in range(lane_tiles):
            place = slice(lane * LANES, (lane + 1) * LANES)
            sums[0:1, place] = jnp.sum(bias_sums[lane], axis=0, keepdims=True)
            sums[1:2, place] = jnp.sum(head_sums[lane], axis=0, keepdims=True)
        sums[2:3, :] = jnp.full((1, hidden), value_total, F32)
        sums[3:8, :] = jnp.zeros((5, hidden), F32)


def first_gradients(flip_of, flags, d_two, w_own, w_other, slope_one, factors, sums, small, d_one):
    count = factors.shape[0]
    hidden = d_two.shape[1]
    small[0 : count + 1, :] = jnp.zeros((count + 1, hidden), F32)
    small[count + 1 : count + 4, :] = sums[0:3, :]
    small[count + 4 : SMALL_ROWS, :] = jnp.zeros((SMALL_ROWS - count - 4, hidden), F32)

    @pl.when(is_active(flags))
    def _():
        flip = flip_of()
        paths = d_two.shape[0]
        width, tile, rows = hidden // 2, 256, 16
        for half, weights in enumerate((w_own, w_other)):
            place = slice(half * width, (half + 1) * width)
            bias_sum = jnp.zeros((8, width), F32)
            for start in range(0, paths, tile):
                d_hidden = lax.dot_general(
                    d_two[start : start + tile, :],
                    weights[...],
                    (((1,), (1,)), ((), ())),
                    preferred_element_type=F32,
                )
                for row in range(0, tile, rows):
                    here = slice(start + row, start + row + rows)
                    d_pre = d_hidden[row : row + rows] * slope_one[here, place].astype(F32)
                    d_one[here, place] = d_pre.astype(BF16)
                    for part in range(0, rows, 8):
                        bias_sum += d_pre[part : part + 8]
            columns = half_columns(flip, half, width)
            small[0:count, columns] = jnp.dot(factors[...], d_one[:, place], preferred_element_type=F32)
            small[count : count + 1, columns] = jnp.sum(bias_sum, axis=0, keepdims=True)


def own_gradient(hidden_one, d_two):
    width = hidden_one.shape[1] // 2
    return lax.dot_general(
        hidden_one[:, :width], d_two[...], (((0,), (0,)), ((), ())), preferred_element_type=F32
    )


def plain_gradient(flags, hidden_one, d_two, grad_own):
    grad_own[...] = jnp.zeros(grad_own.shape, BF16)

    @pl.when(is_active(flags))
    def _():
        grad_own[...] = own_gradient(hidden_one, d_two).astype(BF16)


def half_update(flags, hidden_one, d_two, mom_mid, w_mid, mom_part, w_part):
    def store(momentum):
        mom_part[...] = momentum
        w_part[...] = w_mid[...] - STEP_SIZE * momentum

    @pl.when(is_active(flags))
    def _():
        store(MOMENTUM * mom_mid[...] + own_gradient(hidden_one, d_two))

    @pl.when(jnp.logical_not(is_active(flags)))
    def _():
        store(MOMENTUM * mom_mid[...])


def update(
    paths_total, block, mom_part, w_part, grad_other, small_own, small_other, mom_in, w_in, mom_vec, vec,
    value, new_w_in, new_w_mid, new_vec, new_mom_in, new_mom_mid, new_mom_vec, new_in_copy, new_mid_copy,
    w_in_here, w_mid_here, vec_here, mom_in_here, mom_mid_here, mom_vec_here, in_copy_here, mid_copy_here, sems,
):
    copies = []

    def send(source, target):
        copy = pltpu.make_async_copy(source, target, sems.at[len(copies)])
        copy.start()
        copies.append(copy)

    for start in range(0, mom_part.shape[0], block):
        here = pl.ds(start, block)
        received = grad_other[here, :].astype(F32)
        mom_mid_here[here, :] = mom_part[here, :] + received
        master = w_part[here, :] - STEP_SIZE * received
        w_mid_here[here, :] = master
        mid_copy_here[here, :] = master.astype(BF16)
        send(mom_mid_here.at[here], new_mom_mid.at[here])
        send(w_mid_here.at[here], new_w_mid.at[here])
        send(mid_copy_here.at[here], new_mid_copy.at[here])
    small = small_own[...] + small_other[...]
    count = mom_in.shape[0]
    mom_first = MOMENTUM * mom_in[...] + small[:count]
    first = w_in[...] - STEP_SIZE * mom_first
    mom_in_here[...] = mom_first
    w_in_here[...] = first
    in_copy_here[...] = first.astype(BF16)
    for row in range(3):
        mom_row = MOMENTUM * mom_vec[row] + small[count + row : count + row + 1]
        mom_vec_here[row] = mom_row
        vec_here[row] = vec[row] - STEP_SIZE * mom_row
    send(mom_in_here, new_mom_in)
    send(w_in_here, new_w_in)
    send(in_copy_here, new_in_copy)
    send(mom_vec_here, new_mom_vec)
    send(vec_here, new_vec)
    value[0] = small[count + 3, 0] / paths_total
    for copy in copies:
        copy.wait()


def step_of(mesh):
    levels, cores = mesh.shape["vol"], mesh.shape["path"]
    paired = cores == 2

    def flip_of():
        return lax.axis_index("path") if paired else 0

    def swap(value):
        return lax.ppermute(value, "path", [(0, 1), (1, 0)])

    def shards(
        factors, payoff, terminal, decisions, level_range, w_in_master, w_mid_master, vec_master,
        w_in_copy, w_mid_copy, mom_in, mom_mid, mom_vec,
    ):
        dates, paths = payoff.shape
        count, hidden = w_in_copy.shape[1:]
        width = hidden // 2
        square = 2 * paths * hidden * hidden
        if paired:
            w_own = w_mid_copy[0]
            w_other = swap(w_own)
        else:
            w_full = lax.all_gather(w_mid_copy[0], "path", axis=0, tiled=True)
            w_own, w_other = w_full[:width], w_full[width:]
        vec_hbm = vec_master.transpose(1, 0, 2)
        rows, flags, payoff_near, factors_near, w_in_near, vectors = call(
            prepare,
            (
                shape(dates, paths),
                shape(16, LANES),
                shape(dates, paths),
                shape(count, paths, dtype=BF16),
                shape(count, hidden, dtype=BF16),
                shape(3, 1, hidden),
            ),
            [HBM_SPEC] * 7,
            "prepare",
            0,
            scratch=(
                pltpu.VMEM((1, paths), F32),
                pltpu.VMEM((dates - 1, 1, paths), jnp.int32),
                pltpu.SMEM((2, dates), jnp.int32),
                pltpu.SemaphoreType.DMA((7,)),
            ),
        )(*(far(value) for value in (terminal, decisions, level_range.T, payoff, factors, w_in_copy[0], vec_hbm)))
        lower = [
            lax.ppermute(rows, "vol", [(here, (here + below) % levels) for here in range(levels)])
            for below in range(1, LOWER_LEVELS + 1)
        ]
        hidden_one, slope_one = call(
            lambda *refs: first_layer(flip_of, *refs),
            (shape(paths, hidden, dtype=BF16),) * 2,
            [VMEM_SPEC] * 4,
            "first_layer",
            square,
        )(flags, factors_near, w_in_near, vectors)
        d_two, grad_other, sums = call(
            second_layer,
            (
                shape(paths, hidden, dtype=BF16),
                shape(width, hidden, dtype=BF16),
                shape(8, hidden),
            ),
            [VMEM_SPEC] * 11,
            "second_layer",
            2 * square,
            scratch=(
                pltpu.VMEM((paths, LANES), F32),
                pltpu.VMEM((2, 256, hidden), F32),
                pltpu.VMEM((2, 256, hidden), F32),
                pltpu.VMEM((2, 256, hidden), F32),
                pltpu.VMEM((2, 256, 2 * LANES), BF16),
            ),
        )(flags, hidden_one, w_own, w_other, vectors, payoff_near, rows, *lower)
        if paired:
            grad_other = swap(grad_other)
        (small,) = call(
            lambda *refs: first_gradients(flip_of, *refs),
            (shape(SMALL_ROWS, hidden),),
            [VMEM_SPEC] * 7,
            "first_gradients",
            square,
            scratch=(pltpu.VMEM((paths, hidden), BF16),),
        )(flags, d_two, w_own, w_other, slope_one, factors_near, sums)
        if paired:
            small_other = swap(small)
            mom_part, w_part = call(
                half_update,
                (shape(width, hidden),) * 2,
                [VMEM_SPEC] * 5,
                "half_update",
                square,
            )(flags, hidden_one, d_two, mom_mid[0], w_mid_master[0])
        else:
            (grad_own,) = call(
                plain_gradient,
                (shape(width, hidden, dtype=BF16),),
                [VMEM_SPEC] * 3,
                "plain_gradient",
                square,
            )(flags, hidden_one, d_two)
            grads = jnp.concatenate([grad_own, grad_other])
            grads = lax.psum_scatter(grads, "path", scatter_dimension=0, tiled=True).astype(F32)
            mom_part = MOMENTUM * mom_mid[0] + grads
            w_part = w_mid_master[0] - STEP_SIZE * mom_part
            grad_other = jnp.zeros(grads.shape, BF16)
            small = lax.psum(small, "path")
            small_other = jnp.zeros_like(small)
        own_rows = w_mid_copy.shape[1]
        block = min(128, own_rows)
        outs = (
            shape(1),
            shape(count, hidden),
            shape(own_rows, hidden),
            shape(3, 1, hidden),
            shape(count, hidden),
            shape(own_rows, hidden),
            shape(3, 1, hidden),
            shape(count, hidden, dtype=BF16),
            shape(own_rows, hidden, dtype=BF16),
        )
        value, new_w_in, new_w_mid, new_vec, new_mom_in, new_mom_mid, new_mom_vec, in_copy, mid_copy = call(
            lambda *refs: update(paths * cores, block, *refs),
            outs,
            [VMEM_SPEC] * 9,
            "update",
            0,
            out_specs=[pl.BlockSpec(memory_space=pltpu.SMEM)] + [HBM_SPEC] * 8,
            scratch=[pltpu.VMEM(out.shape, out.dtype) for out in outs[1:]]
            + [pltpu.SemaphoreType.DMA((3 * (own_rows // block) + 5,))],
        )(
            mom_part, w_part, grad_other, small, small_other,
            mom_in[0], w_in_master[0], mom_vec.transpose(1, 0, 2), vectors,
        )
        return (
            value,
            new_w_in[None],
            new_w_mid[None],
            new_vec.transpose(1, 0, 2),
            new_mom_in[None],
            new_mom_mid[None],
            new_mom_vec.transpose(1, 0, 2),
            in_copy[None],
            mid_copy[None],
        )

    return shards


def solution(mesh):
    vectors = P("vol", None, None)
    middle = P("vol", "path", None)
    in_specs = (
        P(None, "path"),
        P(None, "path"),
        P("vol", "path"),
        P(None, "vol", "path"),
        P(),
        vectors,
        middle,
        vectors,
        vectors,
        middle,
        vectors,
        middle,
        vectors,
    )
    out_specs = (P("vol"), vectors, middle, vectors, vectors, middle, vectors, vectors, middle)
    return jax.shard_map(step_of(mesh), mesh=mesh, in_specs=in_specs, out_specs=out_specs, check_vma=False)
```

```python
import jax
import jax.numpy as jnp
from jax import lax
from jax.experimental import pallas as pl
from jax.experimental.pallas import tpu as pltpu
from jax.sharding import PartitionSpec as P

MOMENTUM = 0.9
STEP_SIZE = 0.01
LOWER_LEVELS = 4
SMALL_ROWS = 24
LANES = 128
VMEM_LIMIT = 30 * 1024 * 1024
F32, BF16 = jnp.float32, jnp.bfloat16
VMEM_SPEC = pl.BlockSpec(memory_space=pltpu.VMEM)
HBM_SPEC = pl.BlockSpec(memory_space=pltpu.HBM)


def far(value):
    return pltpu.with_memory_space_constraint(value, pltpu.HBM)


def shape(*dims, dtype=F32):
    return jax.ShapeDtypeStruct(dims, dtype)


def call(kernel, out_shape, in_specs, name, flops, out_specs=None, scratch=()):
    return pl.pallas_call(
        kernel,
        out_shape=out_shape,
        in_specs=in_specs,
        out_specs=out_specs or [VMEM_SPEC] * len(out_shape),
        scratch_shapes=list(scratch),
        compiler_params=pltpu.CompilerParams(vmem_limit_bytes=VMEM_LIMIT),
        cost_estimate=pl.CostEstimate(flops=flops, bytes_accessed=1 << 20, transcendentals=0),
        name=name,
    )


def half_columns(flip, half, width):
    return pl.ds(pl.multiple_of((flip ^ half) * width, width), width)


def is_active(flags):
    return flags[0, 0] > 0.5


def fetch(
    terminal, decisions, ranges, payoff, factors, w_in, vectors,
    terminal_out, decisions_out, payoff_out, factors_out, w_in_out, vectors_out, flags, ranges_here, sems,
):
    copies = [
        pltpu.make_async_copy(source, target, sems.at[index])
        for index, (source, target) in enumerate(
            (
                (ranges, ranges_here),
                (terminal, terminal_out),
                (decisions, decisions_out),
                (payoff, payoff_out),
                (factors, factors_out),
                (w_in, w_in_out),
                (vectors, vectors_out),
            )
        )
    ]
    for copy in copies:
        copy.start()
    copies[0].wait()
    level = lax.axis_index("vol")
    for date in range(payoff.shape[0]):
        low, high = ranges_here[0, date], ranges_here[1, date]
        inside = jnp.logical_and(level >= low, level <= high)
        flags[2 * date : 2 * date + 1, :] = jnp.full((1, LANES), jnp.where(inside, 1.0, 0.0))
        flags[2 * date + 1 : 2 * date + 2, :] = jnp.full((1, LANES), jnp.where(level > high, 1.0, 0.0))
    for copy in copies[1:]:
        copy.wait()


def pack_rows(flags, terminal, decisions, rows):
    dates = rows.shape[0]
    rows[0:1, :] = terminal[...]
    for date in range(dates - 1, 0, -1):
        inside, above = flags[2 * date : 2 * date + 1, 0:1], flags[2 * date + 1 : 2 * date + 2, 0:1]
        rows[dates - date : dates - date + 1, :] = inside * decisions[date - 1].astype(F32) + above


def silu_parts(half):
    bent = jnp.tanh(half)
    upper = 1.0 + bent
    act = half * upper
    return act, upper + act * (1.0 - bent)


def first_layer(flip_of, flags, terminal, decisions, factors, w_in, vectors, rows_out, hidden_one, slope_one):
    pack_rows(flags, terminal, decisions, rows_out)

    @pl.when(is_active(flags))
    def _():
        flip = flip_of()
        hidden = w_in.shape[1]
        width, paths, tile, rows = hidden // 2, factors.shape[1], 256, 16
        for half in range(2):
            columns = half_columns(flip, half, width)
            weights = (0.5 * w_in[:, columns].astype(F32)).astype(BF16)
            bias = 0.5 * vectors[0, :, columns]
            place = slice(half * width, (half + 1) * width)
            for start in range(0, paths, tile):
                pre = lax.dot_general(
                    factors[:, start : start + tile],
                    weights,
                    (((0,), (0,)), ((), ())),
                    preferred_element_type=F32,
                )
                for row in range(0, tile, rows):
                    act, slope = silu_parts(pre[row : row + rows] + bias)
                    here = slice(start + row, start + row + rows)
                    hidden_one[here, place] = act.astype(BF16)
                    slope_one[here, place] = slope


def continuation(level, payoff, row_sets):
    dates = payoff.shape[0]
    conts = [jnp.where(level >= below, rows[0:1, :], 0.0) for below, rows in enumerate(row_sets)]
    for date in range(dates - 1, 0, -1):
        updated = []
        for below in range(len(conts) - 1):
            taken = row_sets[below][dates - date : dates - date + 1, :]
            value = taken * (payoff[date : date + 1, :] + conts[below + 1]) + (1.0 - taken) * conts[below]
            updated.append(jnp.where(level >= below, value, 0.0))
        conts = updated
    return conts


def second_forward(flags, hidden_one, w_own, w_other, vectors, weighted, act_two, logits, parts):
    @pl.when(is_active(flags))
    def _():
        paths, hidden = hidden_one.shape
        width, tile, rows = hidden // 2, 512, 16
        bias, head = 0.5 * vectors[1], vectors[2]
        half_head = 0.5 * head
        for start in range(0, paths, tile):
            here = slice(start, start + tile)
            pre = jnp.dot(hidden_one[here, :width], w_own[...], preferred_element_type=F32)
            pre += jnp.dot(hidden_one[here, width:], w_other[...], preferred_element_type=F32)
            for row in range(0, tile, rows):
                there = slice(start + row, start + row + rows)
                act, slope = silu_parts(0.5 * pre[row : row + rows] + bias)
                weighted[there, :] = slope * half_head
                act_two[there, :] = act
                terms = act * head
                part = terms[:, :LANES]
                for lane in range(LANES, hidden, LANES):
                    part += terms[:, lane : lane + LANES]
                upper = part.astype(BF16)
                parts[there, :LANES] = upper
                parts[there, LANES:] = (part - upper.astype(F32)).astype(BF16)
        ones = jnp.ones((2 * LANES, LANES), BF16)
        logits[...] = jnp.dot(parts[...], ones, preferred_element_type=F32)


def second_gradients(
    flags, hidden_one, weighted, act_two, logits, payoff, own, low4, low3, low2, low1,
    d_two, grad_other, sums, gains,
):
    level = lax.axis_index("vol")
    paths, hidden = hidden_one.shape
    width, rows = hidden // 2, 16
    lane_tiles = hidden // LANES
    row_sets = [ref[...] for ref in (own, low1, low2, low3, low4)]
    cont_here, cont_below = continuation(level, payoff, row_sets)
    gain = payoff[0:1, :] + cont_below - cont_here
    base_value = flags[1, 0] * jnp.sum(gain) + jnp.sum(cont_here)

    @pl.when(jnp.logical_not(is_active(flags)))
    def _():
        grad_other[...] = jnp.zeros(grad_other.shape, BF16)
        sums[...] = jnp.zeros(sums.shape, F32)
        sums[2:3, :] = jnp.full((1, hidden), base_value, F32)

    @pl.when(is_active(flags))
    def _():
        gains[...] = jnp.transpose(jnp.broadcast_to(gain, (LANES, paths)))
        bias_sums = [jnp.zeros((8, LANES), F32) for _ in range(lane_tiles)]
        head_sums = [jnp.zeros((8, LANES), F32) for _ in range(lane_tiles)]
        value_sum = jnp.zeros((rows, LANES), F32)
        for row in range(0, paths, rows):
            here = slice(row, row + rows)
            chance = 0.5 + 0.5 * jnp.tanh(0.5 * logits[here, :])
            weight = gains[here, :] * chance
            value_sum += weight
            d_logit = weight * (chance - 1.0)
            for lane in range(lane_tiles):
                place = slice(lane * LANES, (lane + 1) * LANES)
                d_pre = d_logit * weighted[here, place]
                scaled = d_logit * act_two[here, place]
                d_two[here, place] = d_pre.astype(BF16)
                for part in range(0, rows, 8):
                    bias_sums[lane] += d_pre[part : part + 8]
                    head_sums[lane] += scaled[part : part + 8]
        grad_other[...] = lax.dot_general(
            hidden_one[:, width:], d_two[...], (((0,), (0,)), ((), ())), preferred_element_type=F32
        ).astype(BF16)
        value_total = base_value + jnp.sum(value_sum) / LANES
        for lane in range(lane_tiles):
            place = slice(lane * LANES, (lane + 1) * LANES)
            sums[0:1, place] = jnp.sum(bias_sums[lane], axis=0, keepdims=True)
            sums[1:2, place] = jnp.sum(head_sums[lane], axis=0, keepdims=True)
        sums[2:3, :] = jnp.full((1, hidden), value_total, F32)
        sums[3:8, :] = jnp.zeros((5, hidden), F32)


def first_gradients(flip_of, flags, d_two, w_own, w_other, slope_one, factors, sums, small, d_one):
    count = factors.shape[0]
    hidden = d_two.shape[1]
    small[0 : count + 1, :] = jnp.zeros((count + 1, hidden), F32)
    small[count + 1 : count + 4, :] = sums[0:3, :]
    small[count + 4 : SMALL_ROWS, :] = jnp.zeros((SMALL_ROWS - count - 4, hidden), F32)

    @pl.when(is_active(flags))
    def _():
        flip = flip_of()
        paths = d_two.shape[0]
        width, tile, rows = hidden // 2, 512, 16
        for half, weights in enumerate((w_own, w_other)):
            place = slice(half * width, (half + 1) * width)
            bias_sum = jnp.zeros((8, width), F32)
            for start in range(0, paths, tile):
                d_hidden = lax.dot_general(
                    d_two[start : start + tile, :],
                    weights[...],
                    (((1,), (1,)), ((), ())),
                    preferred_element_type=F32,
                )
                for row in range(0, tile, rows):
                    here = slice(start + row, start + row + rows)
                    d_pre = d_hidden[row : row + rows] * slope_one[here, place]
                    d_one[here, place] = d_pre.astype(BF16)
                    for part in range(0, rows, 8):
                        bias_sum += d_pre[part : part + 8]
            columns = half_columns(flip, half, width)
            small[0:count, columns] = 0.5 * jnp.dot(
                factors[...], d_one[:, place], preferred_element_type=F32
            )
            small[count : count + 1, columns] = 0.5 * jnp.sum(bias_sum, axis=0, keepdims=True)


def own_gradient(hidden_one, d_two, columns):
    return lax.dot_general(
        hidden_one[:, columns], d_two[...], (((0,), (0,)), ((), ())), preferred_element_type=F32
    )


def plain_gradient(flags, hidden_one, d_two, grad_own):
    grad_own[...] = jnp.zeros(grad_own.shape, BF16)

    @pl.when(is_active(flags))
    def _():
        grad_own[...] = own_gradient(hidden_one, d_two, slice(0, grad_own.shape[0])).astype(BF16)


class Sends:
    def __init__(self, sems):
        self.sems, self.copies = sems, []

    def __call__(self, source, target):
        copy = pltpu.make_async_copy(source, target, self.sems.at[len(self.copies)])
        copy.start()
        self.copies.append(copy)

    def finish(self):
        for copy in self.copies:
            copy.wait()


def middle_update(block, paired, flags, *refs):
    if paired:
        hidden_one, d_two, *refs = refs
    grad, mom_mid, w_mid, new_mom, new_w, new_copy, mom_here, w_here, copy_here, sems = refs

    def write(gradient_of):
        sends = Sends(sems)
        for start in range(0, mom_mid.shape[0], block):
            here = pl.ds(start, block)
            momentum = MOMENTUM * mom_mid[here, :] + gradient_of(start, here)
            mom_here[here, :] = momentum
            master = w_mid[here, :] - STEP_SIZE * momentum
            w_here[here, :] = master
            copy_here[here, :] = master.astype(BF16)
            sends(mom_here.at[here], new_mom.at[here])
            sends(w_here.at[here], new_w.at[here])
            sends(copy_here.at[here], new_copy.at[here])
        sends.finish()

    if not paired:
        write(lambda start, here: grad[here, :].astype(F32))
        return

    @pl.when(is_active(flags))
    def _():
        write(
            lambda start, here: own_gradient(hidden_one, d_two, slice(start, start + block))
            + grad[here, :].astype(F32)
        )

    @pl.when(jnp.logical_not(is_active(flags)))
    def _():
        write(lambda start, here: grad[here, :].astype(F32))


def small_update(
    paths_total, after, small_own, small_other, mom_in, w_in, mom_vec, vec,
    value, new_w_in, new_vec, new_mom_in, new_mom_vec, new_copy,
    value_here, w_in_here, vec_here, mom_in_here, mom_vec_here, copy_here, sems,
):
    del after
    sends = Sends(sems)
    small = small_own[...] + small_other[...]
    count = mom_in.shape[0]
    mom_first = MOMENTUM * mom_in[...] + small[:count]
    first = w_in[...] - STEP_SIZE * mom_first
    mom_in_here[...] = mom_first
    w_in_here[...] = first
    copy_here[...] = first.astype(BF16)
    for row in range(3):
        mom_row = MOMENTUM * mom_vec[row] + small[count + row : count + row + 1]
        mom_vec_here[row] = mom_row
        vec_here[row] = vec[row] - STEP_SIZE * mom_row
    sends(mom_in_here, new_mom_in)
    sends(w_in_here, new_w_in)
    sends(copy_here, new_copy)
    sends(mom_vec_here, new_mom_vec)
    sends(vec_here, new_vec)
    value_here[0] = small[count + 3, 0] / paths_total
    sends(value_here, value)
    sends.finish()


def step_of(mesh):
    levels, cores = mesh.shape["vol"], mesh.shape["path"]
    paired = cores == 2

    def flip_of():
        return lax.axis_index("path") if paired else 0

    def swap(value):
        return lax.ppermute(value, "path", [(0, 1), (1, 0)])

    def shards(
        factors, payoff, terminal, decisions, level_range, w_in_master, w_mid_master, vec_master,
        w_in_copy, w_mid_copy, mom_in, mom_mid, mom_vec,
    ):
        dates, paths = payoff.shape
        count, hidden = w_in_copy.shape[1:]
        width = hidden // 2
        square = 2 * paths * hidden * hidden
        if paired:
            w_own = w_mid_copy[0]
            w_other = swap(w_own)
        else:
            w_full = lax.all_gather(w_mid_copy[0], "path", axis=0, tiled=True)
            w_own, w_other = w_full[:width], w_full[width:]
        vec_hbm = vec_master.transpose(1, 0, 2)
        terminal_near, decisions_near, payoff_near, factors_near, w_in_near, vectors, flags = call(
            fetch,
            (
                shape(1, paths),
                shape(dates - 1, 1, paths, dtype=jnp.int32),
                shape(dates, paths),
                shape(count, paths, dtype=BF16),
                shape(count, hidden, dtype=BF16),
                shape(3, 1, hidden),
                shape(2 * dates, LANES),
            ),
            [HBM_SPEC] * 7,
            "fetch",
            0,
            scratch=(pltpu.SMEM((2, dates), jnp.int32), pltpu.SemaphoreType.DMA((7,))),
        )(*(far(value) for value in (terminal, decisions, level_range.T, payoff, factors, w_in_copy[0], vec_hbm)))
        rows, hidden_one, slope_one = call(
            lambda *refs: first_layer(flip_of, *refs),
            (shape(dates, paths), shape(paths, hidden, dtype=BF16), shape(paths, hidden)),
            [VMEM_SPEC] * 6,
            "first_layer",
            square,
        )(flags, terminal_near, decisions_near, factors_near, w_in_near, vectors)
        lower = [
            lax.ppermute(rows, "vol", [(here, (here + below) % levels) for here in range(levels)])
            for below in range(LOWER_LEVELS, 0, -1)
        ][::-1]
        weighted, act_two, logits = call(
            second_forward,
            (shape(paths, hidden), shape(paths, hidden), shape(paths, LANES)),
            [VMEM_SPEC] * 5,
            "second_forward",
            square,
            scratch=(pltpu.VMEM((paths, 2 * LANES), BF16),),
        )(flags, hidden_one, w_own, w_other, vectors)
        d_two, grad_other, sums = call(
            second_gradients,
            (
                shape(paths, hidden, dtype=BF16),
                shape(width, hidden, dtype=BF16),
                shape(8, hidden),
            ),
            [VMEM_SPEC] * 11,
            "second_gradients",
            square,
            scratch=(pltpu.VMEM((paths, LANES), F32),),
        )(flags, hidden_one, weighted, act_two, logits, payoff_near, rows, *lower[::-1])
        if paired:
            grad_other = swap(grad_other)
        (small,) = call(
            lambda *refs: first_gradients(flip_of, *refs),
            (shape(SMALL_ROWS, hidden),),
            [VMEM_SPEC] * 7,
            "first_gradients",
            square,
            scratch=(pltpu.VMEM((paths, hidden), BF16),),
        )(flags, d_two, w_own, w_other, slope_one, factors_near, sums)
        if paired:
            small_other = swap(small)
            gradients = (hidden_one, d_two, grad_other)
        else:
            (grad_own,) = call(
                plain_gradient,
                (shape(width, hidden, dtype=BF16),),
                [VMEM_SPEC] * 3,
                "plain_gradient",
                square,
            )(flags, hidden_one, d_two)
            grads = jnp.concatenate([grad_own, grad_other])
            gradients = (lax.psum_scatter(grads, "path", scatter_dimension=0, tiled=True),)
            small = lax.psum(small, "path")
            small_other = jnp.zeros_like(small)
        own_rows = w_mid_copy.shape[1]
        block = min(128, own_rows)
        outs = (
            shape(own_rows, hidden),
            shape(own_rows, hidden),
            shape(own_rows, hidden, dtype=BF16),
        )
        new_mom_mid, new_w_mid, mid_copy = call(
            lambda *refs: middle_update(block, paired, *refs),
            outs,
            [VMEM_SPEC] * (3 + len(gradients)),
            "middle_update",
            square,
            out_specs=[HBM_SPEC] * 3,
            scratch=[pltpu.VMEM(out.shape, out.dtype) for out in outs]
            + [pltpu.SemaphoreType.DMA((3 * (own_rows // block),))],
        )(flags, *gradients, mom_mid[0], w_mid_master[0])
        outs = (
            shape(1),
            shape(count, hidden),
            shape(3, 1, hidden),
            shape(count, hidden),
            shape(3, 1, hidden),
            shape(count, hidden, dtype=BF16),
        )
        value, new_w_in, new_vec, new_mom_in, new_mom_vec, in_copy = call(
            lambda *refs: small_update(paths * cores, *refs),
            outs,
            [HBM_SPEC] + [VMEM_SPEC] * 6,
            "small_update",
            0,
            out_specs=[HBM_SPEC] * 6,
            scratch=[pltpu.SMEM((1,), F32)]
            + [pltpu.VMEM(out.shape, out.dtype) for out in outs[1:]]
            + [pltpu.SemaphoreType.DMA((6,))],
        )(far(new_mom_mid), small, small_other, mom_in[0], w_in_master[0], mom_vec.transpose(1, 0, 2), vectors)
        return (
            value,
            new_w_in[None],
            new_w_mid[None],
            new_vec.transpose(1, 0, 2),
            new_mom_in[None],
            new_mom_mid[None],
            new_mom_vec.transpose(1, 0, 2),
            in_copy[None],
            mid_copy[None],
        )

    return shards


def solution(mesh):
    vectors = P("vol", None, None)
    middle = P("vol", "path", None)
    in_specs = (
        P(None, "path"),
        P(None, "path"),
        P("vol", "path"),
        P(None, "vol", "path"),
        P(),
        vectors,
        middle,
        vectors,
        vectors,
        middle,
        vectors,
        middle,
        vectors,
    )
    out_specs = (P("vol"), vectors, middle, vectors, vectors, middle, vectors, vectors, middle)
    return jax.shard_map(step_of(mesh), mesh=mesh, in_specs=in_specs, out_specs=out_specs, check_vma=False)
```

```python
import jax
import jax.numpy as jnp
from jax import lax
from jax.experimental import pallas as pl
from jax.experimental.pallas import tpu as pltpu
from jax.sharding import PartitionSpec as P

MOMENTUM = 0.9
STEP_SIZE = 0.01
LOWER_LEVELS = 4
CORE_SHIFTS = ((4, 1), (2, 3))
SMALL_ROWS = 24
LANES = 128
VMEM_LIMIT = 30 * 1024 * 1024
F32, BF16 = jnp.float32, jnp.bfloat16
VMEM_SPEC = pl.BlockSpec(memory_space=pltpu.VMEM)
HBM_SPEC = pl.BlockSpec(memory_space=pltpu.HBM)


def far(value):
    return pltpu.with_memory_space_constraint(value, pltpu.HBM)


def shape(*dims, dtype=F32):
    return jax.ShapeDtypeStruct(dims, dtype)


def call(kernel, out_shape, in_specs, name, flops, out_specs=None, scratch=()):
    return pl.pallas_call(
        kernel,
        out_shape=out_shape,
        in_specs=in_specs,
        out_specs=out_specs or [VMEM_SPEC] * len(out_shape),
        scratch_shapes=list(scratch),
        compiler_params=pltpu.CompilerParams(vmem_limit_bytes=VMEM_LIMIT),
        cost_estimate=pl.CostEstimate(flops=flops, bytes_accessed=1 << 20, transcendentals=0),
        name=name,
    )


def half_columns(flip, half, width):
    return pl.ds(pl.multiple_of((flip ^ half) * width, width), width)


def is_active(flags):
    return flags[0, 0] > 0.5


def fetch(
    terminal, decisions, ranges, payoff, factors, w_in, vectors,
    rows, payoff_out, factors_out, w_in_out, vectors_out, flags,
    terminal_here, decisions_here, ranges_here, sems,
):
    copies = [
        pltpu.make_async_copy(source, target, sems.at[index])
        for index, (source, target) in enumerate(
            (
                (ranges, ranges_here),
                (terminal, terminal_here),
                (decisions, decisions_here),
                (payoff, payoff_out),
                (factors, factors_out),
                (w_in, w_in_out),
                (vectors, vectors_out),
            )
        )
    ]
    for copy in copies:
        copy.start()
    for copy in copies[:3]:
        copy.wait()
    level = lax.axis_index("vol")
    dates = payoff.shape[0]
    rows[0:1, :] = terminal_here[...]
    for date in range(dates):
        low, high = ranges_here[0, date], ranges_here[1, date]
        inside = jnp.where(jnp.logical_and(level >= low, level <= high), 1.0, 0.0)
        above = jnp.where(level > high, 1.0, 0.0)
        if date == 0:
            flags[0:1, :] = jnp.full((1, LANES), inside)
            flags[1:2, :] = jnp.full((1, LANES), above)
        else:
            rows[dates - date : dates - date + 1, :] = inside * decisions_here[date - 1].astype(F32) + above
    for copy in copies[3:]:
        copy.wait()


def silu_parts(half):
    bent = jnp.tanh(half)
    upper = 1.0 + bent
    act = half * upper
    return act, upper + act * (1.0 - bent)


def first_layer(flip_of, flags, rows, factors, w_in, vectors, rows_out, hidden_one, slope_one):
    rows_out[...] = rows[...]

    @pl.when(is_active(flags))
    def _():
        flip = flip_of()
        hidden = w_in.shape[1]
        width, paths, tile, rows = hidden // 2, factors.shape[1], 256, 16
        for half in range(2):
            columns = half_columns(flip, half, width)
            weights = (0.5 * w_in[:, columns].astype(F32)).astype(BF16)
            bias = 0.5 * vectors[0, :, columns]
            place = slice(half * width, (half + 1) * width)
            for start in range(0, paths, tile):
                pre = lax.dot_general(
                    factors[:, start : start + tile],
                    weights,
                    (((0,), (0,)), ((), ())),
                    preferred_element_type=F32,
                )
                for row in range(0, tile, rows):
                    act, slope = silu_parts(pre[row : row + rows] + bias)
                    here = slice(start + row, start + row + rows)
                    hidden_one[here, place] = act.astype(BF16)
                    slope_one[here, place] = slope


def continuation(level, payoff, row_sets):
    dates = payoff.shape[0]
    conts = [jnp.where(level >= below, rows[0:1, :], 0.0) for below, rows in enumerate(row_sets)]
    for date in range(dates - 1, 0, -1):
        updated = []
        for below in range(len(conts) - 1):
            taken = row_sets[below][dates - date : dates - date + 1, :]
            value = taken * (payoff[date : date + 1, :] + conts[below + 1]) + (1.0 - taken) * conts[below]
            updated.append(jnp.where(level >= below, value, 0.0))
        conts = updated
    return conts


def crossing_rows(first, second, after, out):
    del after
    dates = first.shape[0] // 2
    out[:dates, :] = first[dates:, :]
    out[dates:, :] = second[dates:, :]


def second_forward(flags, hidden_one, w_own, w_other, vectors, weighted, act_two, logits, parts):
    @pl.when(is_active(flags))
    def _():
        paths, hidden = hidden_one.shape
        width, tile, rows = hidden // 2, 512, 16
        bias, head = 0.5 * vectors[1], vectors[2]
        half_head = 0.5 * head
        for start in range(0, paths, tile):
            here = slice(start, start + tile)
            pre = jnp.dot(hidden_one[here, :width], w_own[...], preferred_element_type=F32)
            pre += jnp.dot(hidden_one[here, width:], w_other[...], preferred_element_type=F32)
            for row in range(0, tile, rows):
                there = slice(start + row, start + row + rows)
                act, slope = silu_parts(0.5 * pre[row : row + rows] + bias)
                weighted[there, :] = slope * half_head
                act_two[there, :] = act
                terms = act * head
                part = terms[:, :LANES]
                for lane in range(LANES, hidden, LANES):
                    part += terms[:, lane : lane + LANES]
                upper = part.astype(BF16)
                parts[there, :LANES] = upper
                parts[there, LANES:] = (part - upper.astype(F32)).astype(BF16)
        ones = jnp.ones((2 * LANES, LANES), BF16)
        logits[...] = jnp.dot(parts[...], ones, preferred_element_type=F32)


def second_gradients(sets_of, flags, hidden_one, weighted, act_two, logits, payoff, *refs):
    *row_refs, d_two, grad_other, sums, gains = refs
    level = lax.axis_index("vol")
    paths, hidden = hidden_one.shape
    width, rows = hidden // 2, 16
    lane_tiles = hidden // LANES
    cont_here, cont_below = continuation(level, payoff, sets_of(row_refs))
    gain = payoff[0:1, :] + cont_below - cont_here
    base_value = flags[1, 0] * jnp.sum(gain) + jnp.sum(cont_here)

    @pl.when(jnp.logical_not(is_active(flags)))
    def _():
        grad_other[...] = jnp.zeros(grad_other.shape, BF16)
        sums[...] = jnp.zeros(sums.shape, F32)
        sums[2:3, :] = jnp.full((1, hidden), base_value, F32)

    @pl.when(is_active(flags))
    def _():
        gains[...] = jnp.transpose(jnp.broadcast_to(gain, (LANES, paths)))
        bias_sums = [jnp.zeros((8, LANES), F32) for _ in range(lane_tiles)]
        head_sums = [jnp.zeros((8, LANES), F32) for _ in range(lane_tiles)]
        value_sum = jnp.zeros((rows, LANES), F32)
        for row in range(0, paths, rows):
            here = slice(row, row + rows)
            chance = 0.5 + 0.5 * jnp.tanh(0.5 * logits[here, :])
            weight = gains[here, :] * chance
            value_sum += weight
            d_logit = weight * (chance - 1.0)
            for lane in range(lane_tiles):
                place = slice(lane * LANES, (lane + 1) * LANES)
                d_pre = d_logit * weighted[here, place]
                scaled = d_logit * act_two[here, place]
                d_two[here, place] = d_pre.astype(BF16)
                for part in range(0, rows, 8):
                    bias_sums[lane] += d_pre[part : part + 8]
                    head_sums[lane] += scaled[part : part + 8]
        grad_other[...] = lax.dot_general(
            hidden_one[:, width:], d_two[...], (((0,), (0,)), ((), ())), preferred_element_type=F32
        ).astype(BF16)
        value_total = base_value + jnp.sum(value_sum) / LANES
        for lane in range(lane_tiles):
            place = slice(lane * LANES, (lane + 1) * LANES)
            sums[0:1, place] = jnp.sum(bias_sums[lane], axis=0, keepdims=True)
            sums[1:2, place] = jnp.sum(head_sums[lane], axis=0, keepdims=True)
        sums[2:3, :] = jnp.full((1, hidden), value_total, F32)
        sums[3:8, :] = jnp.zeros((5, hidden), F32)


def first_gradients(flip_of, flags, d_two, w_own, w_other, slope_one, factors, sums, small, d_one):
    count = factors.shape[0]
    hidden = d_two.shape[1]
    small[0 : count + 1, :] = jnp.zeros((count + 1, hidden), F32)
    small[count + 1 : count + 4, :] = sums[0:3, :]
    small[count + 4 : SMALL_ROWS, :] = jnp.zeros((SMALL_ROWS - count - 4, hidden), F32)

    @pl.when(is_active(flags))
    def _():
        flip = flip_of()
        paths = d_two.shape[0]
        width, tile, rows = hidden // 2, 512, 16
        for half, weights in enumerate((w_own, w_other)):
            place = slice(half * width, (half + 1) * width)
            bias_sum = jnp.zeros((8, width), F32)
            for start in range(0, paths, tile):
                d_hidden = lax.dot_general(
                    d_two[start : start + tile, :],
                    weights[...],
                    (((1,), (1,)), ((), ())),
                    preferred_element_type=F32,
                )
                for row in range(0, tile, rows):
                    here = slice(start + row, start + row + rows)
                    d_pre = d_hidden[row : row + rows] * slope_one[here, place]
                    d_one[here, place] = d_pre.astype(BF16)
                    for part in range(0, rows, 8):
                        bias_sum += d_pre[part : part + 8]
            columns = half_columns(flip, half, width)
            small[0:count, columns] = 0.5 * jnp.dot(
                factors[...], d_one[:, place], preferred_element_type=F32
            )
            small[count : count + 1, columns] = 0.5 * jnp.sum(bias_sum, axis=0, keepdims=True)


def own_gradient(hidden_one, d_two, columns):
    return lax.dot_general(
        hidden_one[:, columns], d_two[...], (((0,), (0,)), ((), ())), preferred_element_type=F32
    )


def plain_gradient(flags, hidden_one, d_two, grad_own):
    grad_own[...] = jnp.zeros(grad_own.shape, BF16)

    @pl.when(is_active(flags))
    def _():
        grad_own[...] = own_gradient(hidden_one, d_two, slice(0, grad_own.shape[0])).astype(BF16)


class Sends:
    def __init__(self, sems):
        self.sems, self.copies = sems, []

    def __call__(self, source, target):
        copy = pltpu.make_async_copy(source, target, self.sems.at[len(self.copies)])
        copy.start()
        self.copies.append(copy)

    def finish(self):
        for copy in self.copies:
            copy.wait()


def middle_update(block, paired, flags, *refs):
    if paired:
        hidden_one, d_two, *refs = refs
    grad, mom_mid, w_mid, new_mom, new_w, new_copy, mom_here, w_here, copy_here, sems = refs

    def write(gradient_of):
        sends = Sends(sems)
        for start in range(0, mom_mid.shape[0], block):
            here = pl.ds(start, block)
            momentum = MOMENTUM * mom_mid[here, :] + gradient_of(start, here)
            mom_here[here, :] = momentum
            master = w_mid[here, :] - STEP_SIZE * momentum
            w_here[here, :] = master
            copy_here[here, :] = master.astype(BF16)
            sends(mom_here.at[here], new_mom.at[here])
            sends(w_here.at[here], new_w.at[here])
            sends(copy_here.at[here], new_copy.at[here])
        sends.finish()

    if not paired:
        write(lambda start, here: grad[here, :].astype(F32))
        return

    @pl.when(is_active(flags))
    def _():
        write(
            lambda start, here: own_gradient(hidden_one, d_two, slice(start, start + block))
            + grad[here, :].astype(F32)
        )

    @pl.when(jnp.logical_not(is_active(flags)))
    def _():
        write(lambda start, here: grad[here, :].astype(F32))


def small_update(
    paths_total, after, small_own, small_other, mom_in, w_in, mom_vec, vec,
    value, new_w_in, new_vec, new_mom_in, new_mom_vec, new_copy,
    value_here, w_in_here, vec_here, mom_in_here, mom_vec_here, copy_here, sems,
):
    del after
    sends = Sends(sems)
    small = small_own[...] + small_other[...]
    count = mom_in.shape[0]
    mom_first = MOMENTUM * mom_in[...] + small[:count]
    first = w_in[...] - STEP_SIZE * mom_first
    mom_in_here[...] = mom_first
    w_in_here[...] = first
    copy_here[...] = first.astype(BF16)
    for row in range(3):
        mom_row = MOMENTUM * mom_vec[row] + small[count + row : count + row + 1]
        mom_vec_here[row] = mom_row
        vec_here[row] = vec[row] - STEP_SIZE * mom_row
    sends(mom_in_here, new_mom_in)
    sends(w_in_here, new_w_in)
    sends(copy_here, new_copy)
    sends(mom_vec_here, new_mom_vec)
    sends(vec_here, new_vec)
    value_here[0] = small[count + 3, 0] / paths_total
    sends(value_here, value)
    sends.finish()


def step_of(mesh):
    levels, cores = mesh.shape["vol"], mesh.shape["path"]
    paired = cores == 2

    def flip_of():
        return lax.axis_index("path") if paired else 0

    def swap(value):
        return lax.ppermute(value, "path", [(0, 1), (1, 0)])

    def shards(
        factors, payoff, terminal, decisions, level_range, w_in_master, w_mid_master, vec_master,
        w_in_copy, w_mid_copy, mom_in, mom_mid, mom_vec,
    ):
        dates, paths = payoff.shape
        count, hidden = w_in_copy.shape[1:]
        width = hidden // 2
        square = 2 * paths * hidden * hidden
        if paired:
            w_own = w_mid_copy[0]
            w_other = swap(w_own)
        else:
            w_full = lax.all_gather(w_mid_copy[0], "path", axis=0, tiled=True)
            w_own, w_other = w_full[:width], w_full[width:]
        vec_hbm = vec_master.transpose(1, 0, 2)
        rows, payoff_near, factors_near, w_in_near, vectors, flags = call(
            fetch,
            (
                shape(dates, paths),
                shape(dates, paths),
                shape(count, paths, dtype=BF16),
                shape(count, hidden, dtype=BF16),
                shape(3, 1, hidden),
                shape(8, LANES),
            ),
            [HBM_SPEC] * 7,
            "fetch",
            0,
            scratch=(
                pltpu.VMEM((1, paths), F32),
                pltpu.VMEM((dates - 1, 1, paths), jnp.int32),
                pltpu.SMEM((2, dates), jnp.int32),
                pltpu.SemaphoreType.DMA((7,)),
            ),
        )(*(far(value) for value in (terminal, decisions, level_range.T, payoff, factors, w_in_copy[0], vec_hbm)))

        rows_after, hidden_one, slope_one = call(
            lambda *refs: first_layer(flip_of, *refs),
            (shape(dates, paths), shape(paths, hidden, dtype=BF16), shape(paths, hidden)),
            [VMEM_SPEC] * 5,
            "first_layer",
            square,
        )(flags, rows, factors_near, w_in_near, vectors)
        if paired:
            both = jnp.concatenate([rows_after, swap(rows)])
            lower = [
                lax.ppermute(
                    both,
                    ("vol", "path"),
                    [
                        (here * 2 + core, (here + below[core]) % levels * 2 + core)
                        for here in range(levels)
                        for core in range(2)
                    ],
                )
                for below in CORE_SHIFTS
            ]
        else:
            row_arrays = (rows,) + tuple(
                lax.ppermute(rows, "vol", [(here, (here + below) % levels) for here in range(levels)])
                for below in range(1, LOWER_LEVELS + 1)
            )

        def sets_of(refs):
            if not paired:
                return [ref[...] for ref in refs]
            own, first, second, other = (ref[...] for ref in refs)
            even = lax.axis_index("path") == 0
            sets = {0: own}
            for (low, high), direct, crossing in zip(
                CORE_SHIFTS, (first[:dates], second[:dates]), (other[:dates], other[dates:])
            ):
                sets[low] = jnp.where(even, direct, crossing)
                sets[high] = jnp.where(even, crossing, direct)
            return [sets[below] for below in range(LOWER_LEVELS + 1)]

        weighted, act_two, logits = call(
            second_forward,
            (shape(paths, hidden), shape(paths, hidden), shape(paths, LANES)),
            [VMEM_SPEC] * 5,
            "second_forward",
            square,
            scratch=(pltpu.VMEM((paths, 2 * LANES), BF16),),
        )(flags, hidden_one, w_own, w_other, vectors)
        if paired:
            (crossing,) = call(
                crossing_rows, (shape(2 * dates, paths),), [VMEM_SPEC] * 3, "crossing_rows", 0
            )(*lower, logits)
            row_arrays = (rows, *lower, swap(crossing))
        d_two, grad_other, sums = call(
            lambda *refs: second_gradients(sets_of, *refs),
            (
                shape(paths, hidden, dtype=BF16),
                shape(width, hidden, dtype=BF16),
                shape(8, hidden),
            ),
            [VMEM_SPEC] * (6 + len(row_arrays)),
            "second_gradients",
            square,
            scratch=(pltpu.VMEM((paths, LANES), F32),),
        )(flags, hidden_one, weighted, act_two, logits, payoff_near, *row_arrays)
        if paired:
            grad_other = swap(grad_other)
        (small,) = call(
            lambda *refs: first_gradients(flip_of, *refs),
            (shape(SMALL_ROWS, hidden),),
            [VMEM_SPEC] * 7,
            "first_gradients",
            square,
            scratch=(pltpu.VMEM((paths, hidden), BF16),),
        )(flags, d_two, w_own, w_other, slope_one, factors_near, sums)
        if paired:
            small_other = swap(small)
            gradients = (hidden_one, d_two, grad_other)
        else:
            (grad_own,) = call(
                plain_gradient,
                (shape(width, hidden, dtype=BF16),),
                [VMEM_SPEC] * 3,
                "plain_gradient",
                square,
            )(flags, hidden_one, d_two)
            grads = jnp.concatenate([grad_own, grad_other])
            gradients = (lax.psum_scatter(grads, "path", scatter_dimension=0, tiled=True),)
            small = lax.psum(small, "path")
            small_other = jnp.zeros_like(small)
        own_rows = w_mid_copy.shape[1]
        block = min(128, own_rows)
        outs = (
            shape(own_rows, hidden),
            shape(own_rows, hidden),
            shape(own_rows, hidden, dtype=BF16),
        )
        new_mom_mid, new_w_mid, mid_copy = call(
            lambda *refs: middle_update(block, paired, *refs),
            outs,
            [VMEM_SPEC] * (3 + len(gradients)),
            "middle_update",
            square,
            out_specs=[HBM_SPEC] * 3,
            scratch=[pltpu.VMEM(out.shape, out.dtype) for out in outs]
            + [pltpu.SemaphoreType.DMA((3 * (own_rows // block),))],
        )(flags, *gradients, mom_mid[0], w_mid_master[0])
        outs = (
            shape(1),
            shape(count, hidden),
            shape(3, 1, hidden),
            shape(count, hidden),
            shape(3, 1, hidden),
            shape(count, hidden, dtype=BF16),
        )
        value, new_w_in, new_vec, new_mom_in, new_mom_vec, in_copy = call(
            lambda *refs: small_update(paths * cores, *refs),
            outs,
            [HBM_SPEC] + [VMEM_SPEC] * 6,
            "small_update",
            0,
            out_specs=[HBM_SPEC] * 6,
            scratch=[pltpu.SMEM((1,), F32)]
            + [pltpu.VMEM(out.shape, out.dtype) for out in outs[1:]]
            + [pltpu.SemaphoreType.DMA((6,))],
        )(far(new_mom_mid), small, small_other, mom_in[0], w_in_master[0], mom_vec.transpose(1, 0, 2), vectors)
        return (
            value,
            new_w_in[None],
            new_w_mid[None],
            new_vec.transpose(1, 0, 2),
            new_mom_in[None],
            new_mom_mid[None],
            new_mom_vec.transpose(1, 0, 2),
            in_copy[None],
            mid_copy[None],
        )

    return shards


def solution(mesh):
    vectors = P("vol", None, None)
    middle = P("vol", "path", None)
    in_specs = (
        P(None, "path"),
        P(None, "path"),
        P("vol", "path"),
        P(None, "vol", "path"),
        P(),
        vectors,
        middle,
        vectors,
        vectors,
        middle,
        vectors,
        middle,
        vectors,
    )
    out_specs = (P("vol"), vectors, middle, vectors, vectors, middle, vectors, vectors, middle)
    return jax.shard_map(step_of(mesh), mesh=mesh, in_specs=in_specs, out_specs=out_specs, check_vma=False)
```

```python
import jax
import jax.numpy as jnp
from jax import lax
from jax.experimental import pallas as pl
from jax.experimental.pallas import tpu as pltpu
from jax.sharding import PartitionSpec as P

MOMENTUM = 0.9
STEP_SIZE = 0.01
LOWER_LEVELS = 4
CORE_SHIFTS = ((4, 3), (2, 1))
SMALL_ROWS = 24
LANES = 128
VMEM_LIMIT = 30 * 1024 * 1024
F32, BF16 = jnp.float32, jnp.bfloat16
VMEM_SPEC = pl.BlockSpec(memory_space=pltpu.VMEM)
HBM_SPEC = pl.BlockSpec(memory_space=pltpu.HBM)


def far(value):
    return pltpu.with_memory_space_constraint(value, pltpu.HBM)


def shape(*dims, dtype=F32):
    return jax.ShapeDtypeStruct(dims, dtype)


def call(kernel, out_shape, in_specs, name, flops, out_specs=None, scratch=()):
    return pl.pallas_call(
        kernel,
        out_shape=out_shape,
        in_specs=in_specs,
        out_specs=out_specs or [VMEM_SPEC] * len(out_shape),
        scratch_shapes=list(scratch),
        compiler_params=pltpu.CompilerParams(vmem_limit_bytes=VMEM_LIMIT),
        cost_estimate=pl.CostEstimate(flops=flops, bytes_accessed=1 << 20, transcendentals=0),
        name=name,
    )


def half_columns(flip, half, width):
    return pl.ds(pl.multiple_of((flip ^ half) * width, width), width)


def is_active(flags):
    return flags[0, 0] > 0.5


def fetch(
    terminal, decisions, ranges, payoff, factors, w_in, vectors,
    rows, payoff_out, factors_out, w_in_out, vectors_out, flags,
    terminal_here, decisions_here, ranges_here, sems,
):
    copies = [
        pltpu.make_async_copy(source, target, sems.at[index])
        for index, (source, target) in enumerate(
            (
                (ranges, ranges_here),
                (terminal, terminal_here),
                (decisions, decisions_here),
                (payoff, payoff_out),
                (factors, factors_out),
                (w_in, w_in_out),
                (vectors, vectors_out),
            )
        )
    ]
    for copy in copies:
        copy.start()
    for copy in copies[:3]:
        copy.wait()
    level = lax.axis_index("vol")
    dates = payoff.shape[0]
    rows[0:1, :] = terminal_here[...]
    for date in range(dates):
        low, high = ranges_here[0, date], ranges_here[1, date]
        inside = jnp.where(jnp.logical_and(level >= low, level <= high), 1.0, 0.0)
        above = jnp.where(level > high, 1.0, 0.0)
        if date == 0:
            flags[0:1, :] = jnp.full((1, LANES), inside)
            flags[1:2, :] = jnp.full((1, LANES), above)
        else:
            rows[dates - date : dates - date + 1, :] = inside * decisions_here[date - 1].astype(F32) + above
    for copy in copies[3:]:
        copy.wait()


def silu_parts(half):
    bent = jnp.tanh(half)
    upper = 1.0 + bent
    act = half * upper
    return act, upper + act * (1.0 - bent)


def first_layer(flip_of, flags, rows, factors, w_in, vectors, rows_out, hidden_one, slope_one):
    rows_out[...] = rows[...]

    @pl.when(is_active(flags))
    def _():
        flip = flip_of()
        hidden = w_in.shape[1]
        width, paths, tile, rows = hidden // 2, factors.shape[1], 256, 16
        for half in range(2):
            columns = half_columns(flip, half, width)
            weights = (0.5 * w_in[:, columns].astype(F32)).astype(BF16)
            bias = 0.5 * vectors[0, :, columns]
            place = slice(half * width, (half + 1) * width)
            for start in range(0, paths, tile):
                pre = lax.dot_general(
                    factors[:, start : start + tile],
                    weights,
                    (((0,), (0,)), ((), ())),
                    preferred_element_type=F32,
                )
                for row in range(0, tile, rows):
                    half_pre = pre[row : row + rows] + bias
                    bent = jnp.tanh(half_pre)
                    squash = 0.5 + 0.5 * bent
                    half_act = half_pre * squash
                    here = slice(start + row, start + row + rows)
                    hidden_one[here, place] = half_act.astype(BF16)
                    slope_one[here, place] = squash + half_act * (1.0 - bent)


def continuation(level, payoff, row_sets):
    dates = payoff.shape[0]
    conts = [jnp.where(level >= below, rows[0:1, :], 0.0) for below, rows in enumerate(row_sets)]
    for date in range(dates - 1, 0, -1):
        updated = []
        for below in range(len(conts) - 1):
            taken = row_sets[below][dates - date : dates - date + 1, :]
            value = taken * (payoff[date : date + 1, :] + conts[below + 1]) + (1.0 - taken) * conts[below]
            updated.append(jnp.where(level >= below, value, 0.0))
        conts = updated
    return conts


def crossing_rows(first, second, after, out):
    del after
    start = 0
    for value in (first, second):
        count = value.shape[0] // 2
        out[start : start + count, :] = value[count:, :]
        start += count


def second_forward(flags, hidden_one, w_own, w_other, vectors, weighted, act_two, partial, joined):
    @pl.when(is_active(flags))
    def _():
        paths, hidden = hidden_one.shape
        width, rows = hidden // 2, 8
        bias, head = 0.5 * vectors[1], vectors[2]
        half_head = 0.5 * head
        joined[:width, :] = w_own[...]
        joined[width:, :] = w_other[...]
        pre = jnp.dot(hidden_one[...], joined[...], preferred_element_type=F32)
        for row in range(0, paths, rows):
            here = slice(row, row + rows)
            act, slope = silu_parts(pre[here] + bias)
            weighted[here, :] = slope * half_head
            act_two[here, :] = act
            terms = act * head
            part = terms[:, :LANES]
            for lane in range(LANES, hidden, LANES):
                part += terms[:, lane : lane + LANES]
            partial[here, :] = part


def exercise_chance(flags, partial, after, chance, parts):
    del after

    @pl.when(is_active(flags))
    def _():
        paths, rows = partial.shape[0], 16
        for row in range(0, paths, rows):
            here = slice(row, row + rows)
            part = partial[here, :]
            upper = part.astype(BF16)
            parts[here, :LANES] = upper
            parts[here, LANES:] = (part - upper.astype(F32)).astype(BF16)
        ones = jnp.ones((2 * LANES, LANES), BF16)
        logits = jnp.dot(parts[...], ones, preferred_element_type=F32)
        chance[...] = 0.5 + 0.5 * jnp.tanh(0.5 * logits)


def second_gradients(sets_of, flags, hidden_one, weighted, act_two, chances, payoff, *refs):
    *row_refs, d_two, grad_other, sums, gains = refs
    level = lax.axis_index("vol")
    paths, hidden = hidden_one.shape
    width, rows = hidden // 2, 16
    lane_tiles = hidden // LANES
    cont_here, cont_below = continuation(level, payoff, sets_of(row_refs))
    gain = payoff[0:1, :] + cont_below - cont_here
    base_value = flags[1, 0] * jnp.sum(gain) + jnp.sum(cont_here)

    @pl.when(jnp.logical_not(is_active(flags)))
    def _():
        grad_other[...] = jnp.zeros(grad_other.shape, BF16)
        sums[...] = jnp.zeros(sums.shape, F32)
        sums[2:3, :] = jnp.full((1, hidden), base_value, F32)

    @pl.when(is_active(flags))
    def _():
        gains[...] = jnp.transpose(jnp.broadcast_to(gain, (LANES, paths)))
        bias_sums = [jnp.zeros((8, LANES), F32) for _ in range(lane_tiles)]
        head_sums = [jnp.zeros((8, LANES), F32) for _ in range(lane_tiles)]
        value_sum = jnp.zeros((rows, LANES), F32)
        for row in range(0, paths, rows):
            here = slice(row, row + rows)
            chance = chances[here, :]
            weight = gains[here, :] * chance
            value_sum += weight
            d_logit = weight * (chance - 1.0)
            for lane in range(lane_tiles):
                place = slice(lane * LANES, (lane + 1) * LANES)
                d_pre = d_logit * weighted[here, place]
                scaled = d_logit * act_two[here, place]
                d_two[here, place] = d_pre.astype(BF16)
                for part in range(0, rows, 8):
                    bias_sums[lane] += d_pre[part : part + 8]
                    head_sums[lane] += scaled[part : part + 8]
        grad_other[...] = lax.dot_general(
            hidden_one[:, width:], d_two[...], (((0,), (0,)), ((), ())), preferred_element_type=F32
        ).astype(BF16)
        value_total = base_value + jnp.sum(value_sum) / LANES
        for lane in range(lane_tiles):
            place = slice(lane * LANES, (lane + 1) * LANES)
            sums[0:1, place] = jnp.sum(bias_sums[lane], axis=0, keepdims=True)
            sums[1:2, place] = jnp.sum(head_sums[lane], axis=0, keepdims=True)
        sums[2:3, :] = jnp.full((1, hidden), value_total, F32)
        sums[3:8, :] = jnp.zeros((5, hidden), F32)


def first_gradients(flip_of, flags, d_two, w_own, w_other, slope_one, factors, sums, small, d_one):
    count = factors.shape[0]
    hidden = d_two.shape[1]
    small[0 : count + 1, :] = jnp.zeros((count + 1, hidden), F32)
    small[count + 1 : count + 4, :] = sums[0:3, :]
    small[count + 4 : SMALL_ROWS, :] = jnp.zeros((SMALL_ROWS - count - 4, hidden), F32)

    @pl.when(is_active(flags))
    def _():
        flip = flip_of()
        paths = d_two.shape[0]
        width, tile, rows = hidden // 2, 512, 16
        for half, weights in enumerate((w_own, w_other)):
            place = slice(half * width, (half + 1) * width)
            bias_sum = jnp.zeros((8, width), F32)
            for start in range(0, paths, tile):
                d_hidden = lax.dot_general(
                    d_two[start : start + tile, :],
                    weights[...],
                    (((1,), (1,)), ((), ())),
                    preferred_element_type=F32,
                )
                for row in range(0, tile, rows):
                    here = slice(start + row, start + row + rows)
                    d_pre = d_hidden[row : row + rows] * slope_one[here, place]
                    d_one[here, place] = d_pre.astype(BF16)
                    for part in range(0, rows, 8):
                        bias_sum += d_pre[part : part + 8]
            columns = half_columns(flip, half, width)
            small[0:count, columns] = jnp.dot(factors[...], d_one[:, place], preferred_element_type=F32)
            small[count : count + 1, columns] = jnp.sum(bias_sum, axis=0, keepdims=True)


def own_gradient(hidden_one, d_two, columns):
    return lax.dot_general(
        hidden_one[:, columns], d_two[...], (((0,), (0,)), ((), ())), preferred_element_type=F32
    )


def plain_gradient(flags, hidden_one, d_two, grad_own):
    grad_own[...] = jnp.zeros(grad_own.shape, BF16)

    @pl.when(is_active(flags))
    def _():
        grad_own[...] = own_gradient(hidden_one, d_two, slice(0, grad_own.shape[0])).astype(BF16)


class Sends:
    def __init__(self, sems):
        self.sems, self.copies = sems, []

    def __call__(self, source, target):
        copy = pltpu.make_async_copy(source, target, self.sems.at[len(self.copies)])
        copy.start()
        self.copies.append(copy)

    def finish(self):
        for copy in self.copies:
            copy.wait()


def middle_update(block, paired, flags, *refs):
    if paired:
        hidden_one, d_two, *refs = refs
    grad, mom_mid, w_mid, new_mom, new_w, new_copy, mom_here, w_here, copy_here, sems = refs

    def write(gradient_of):
        sends = Sends(sems)
        for start in range(0, mom_mid.shape[0], block):
            here = pl.ds(start, block)
            momentum = MOMENTUM * mom_mid[here, :] + 2.0 * gradient_of(start, here)
            mom_here[here, :] = momentum
            master = w_mid[here, :] - STEP_SIZE * momentum
            w_here[here, :] = master
            copy_here[here, :] = master.astype(BF16)
            sends(mom_here.at[here], new_mom.at[here])
            sends(w_here.at[here], new_w.at[here])
            sends(copy_here.at[here], new_copy.at[here])
        sends.finish()

    if not paired:
        write(lambda start, here: grad[here, :].astype(F32))
        return

    @pl.when(is_active(flags))
    def _():
        write(
            lambda start, here: own_gradient(hidden_one, d_two, slice(start, start + block))
            + grad[here, :].astype(F32)
        )

    @pl.when(jnp.logical_not(is_active(flags)))
    def _():
        write(lambda start, here: grad[here, :].astype(F32))


def small_update(
    paths_total, after, small_own, small_other, mom_in, w_in, mom_vec, vec,
    value, new_w_in, new_vec, new_mom_in, new_mom_vec, new_copy,
    value_here, w_in_here, vec_here, mom_in_here, mom_vec_here, copy_here, sems,
):
    del after
    sends = Sends(sems)
    small = small_own[...] + small_other[...]
    count = mom_in.shape[0]
    mom_first = MOMENTUM * mom_in[...] + small[:count]
    first = w_in[...] - STEP_SIZE * mom_first
    mom_in_here[...] = mom_first
    w_in_here[...] = first
    copy_here[...] = first.astype(BF16)
    for row in range(3):
        mom_row = MOMENTUM * mom_vec[row] + small[count + row : count + row + 1]
        mom_vec_here[row] = mom_row
        vec_here[row] = vec[row] - STEP_SIZE * mom_row
    sends(mom_in_here, new_mom_in)
    sends(w_in_here, new_w_in)
    sends(copy_here, new_copy)
    sends(mom_vec_here, new_mom_vec)
    sends(vec_here, new_vec)
    value_here[0] = small[count + 3, 0] / paths_total
    sends(value_here, value)
    sends.finish()


def step_of(mesh):
    levels, cores = mesh.shape["vol"], mesh.shape["path"]
    paired = cores == 2

    def flip_of():
        return lax.axis_index("path") if paired else 0

    def swap(value):
        return lax.ppermute(value, "path", [(0, 1), (1, 0)])

    def shards(
        factors, payoff, terminal, decisions, level_range, w_in_master, w_mid_master, vec_master,
        w_in_copy, w_mid_copy, mom_in, mom_mid, mom_vec,
    ):
        dates, paths = payoff.shape
        count, hidden = w_in_copy.shape[1:]
        width = hidden // 2
        square = 2 * paths * hidden * hidden
        if paired:
            w_own = w_mid_copy[0]
            w_other = swap(w_own)
        else:
            w_full = lax.all_gather(w_mid_copy[0], "path", axis=0, tiled=True)
            w_own, w_other = w_full[:width], w_full[width:]
        vec_hbm = vec_master.transpose(1, 0, 2)
        rows, payoff_near, factors_near, w_in_near, vectors, flags = call(
            fetch,
            (
                shape(dates, paths),
                shape(dates, paths),
                shape(count, paths, dtype=BF16),
                shape(count, hidden, dtype=BF16),
                shape(3, 1, hidden),
                shape(8, LANES),
            ),
            [HBM_SPEC] * 7,
            "fetch",
            0,
            scratch=(
                pltpu.VMEM((1, paths), F32),
                pltpu.VMEM((dates - 1, 1, paths), jnp.int32),
                pltpu.SMEM((2, dates), jnp.int32),
                pltpu.SemaphoreType.DMA((7,)),
            ),
        )(*(far(value) for value in (terminal, decisions, level_range.T, payoff, factors, w_in_copy[0], vec_hbm)))

        rows_after, hidden_one, slope_one = call(
            lambda *refs: first_layer(flip_of, *refs),
            (shape(dates, paths), shape(paths, hidden, dtype=BF16), shape(paths, hidden)),
            [VMEM_SPEC] * 5,
            "first_layer",
            square,
        )(flags, rows, factors_near, w_in_near, vectors)
        if paired:
            both = jnp.concatenate([rows_after, swap(rows)])
            lower = [
                lax.ppermute(
                    both,
                    ("vol", "path"),
                    [
                        (here * 2 + core, (here + below[core]) % levels * 2 + core)
                        for here in range(levels)
                        for core in range(2)
                    ],
                )
                for below in CORE_SHIFTS
            ]
        else:
            row_arrays = (rows,) + tuple(
                lax.ppermute(rows, "vol", [(here, (here + below) % levels) for here in range(levels)])
                for below in range(1, LOWER_LEVELS + 1)
            )

        def sets_of(refs):
            if not paired:
                return [ref[...] for ref in refs]
            own, *lower, crossing = (ref[...] for ref in refs)
            even = lax.axis_index("path") == 0
            sets, start = {0: own}, 0
            for (low, high), value in zip(CORE_SHIFTS, lower):
                size = value.shape[0] // 2
                direct, crossed = value[:size], crossing[start : start + size]
                sets[low] = jnp.where(even, direct, crossed)
                sets[high] = jnp.where(even, crossed, direct)
                start += size
            return [sets[below] for below in range(LOWER_LEVELS + 1)]

        weighted, act_two, partial = call(
            second_forward,
            (shape(paths, hidden), shape(paths, hidden), shape(paths, LANES)),
            [VMEM_SPEC] * 5,
            "second_forward",
            square,
            scratch=(pltpu.VMEM((hidden, hidden), BF16),),
        )(flags, hidden_one, w_own, w_other, vectors)
        after = partial
        if paired:
            crossed = sum(value.shape[0] for value in lower) // 2
            (after,) = call(
                crossing_rows, (shape(crossed, paths),), [VMEM_SPEC] * 3, "crossing_rows", 0
            )(*lower, partial)
            row_arrays = (rows, *lower, swap(after))
        (chances,) = call(
            exercise_chance,
            (shape(paths, LANES),),
            [VMEM_SPEC] * 3,
            "exercise_chance",
            square,
            scratch=(pltpu.VMEM((paths, 2 * LANES), BF16),),
        )(flags, partial, after)
        d_two, grad_other, sums = call(
            lambda *refs: second_gradients(sets_of, *refs),
            (
                shape(paths, hidden, dtype=BF16),
                shape(width, hidden, dtype=BF16),
                shape(8, hidden),
            ),
            [VMEM_SPEC] * (6 + len(row_arrays)),
            "second_gradients",
            square,
            scratch=(pltpu.VMEM((paths, LANES), F32),),
        )(flags, hidden_one, weighted, act_two, chances, payoff_near, *row_arrays)
        if paired:
            grad_other = swap(grad_other)
        (small,) = call(
            lambda *refs: first_gradients(flip_of, *refs),
            (shape(SMALL_ROWS, hidden),),
            [VMEM_SPEC] * 7,
            "first_gradients",
            square,
            scratch=(pltpu.VMEM((paths, hidden), BF16),),
        )(flags, d_two, w_own, w_other, slope_one, factors_near, sums)
        if paired:
            small_other = swap(small)
            gradients = (hidden_one, d_two, grad_other)
        else:
            (grad_own,) = call(
                plain_gradient,
                (shape(width, hidden, dtype=BF16),),
                [VMEM_SPEC] * 3,
                "plain_gradient",
                square,
            )(flags, hidden_one, d_two)
            grads = jnp.concatenate([grad_own, grad_other])
            gradients = (lax.psum_scatter(grads, "path", scatter_dimension=0, tiled=True),)
            small = lax.psum(small, "path")
            small_other = jnp.zeros_like(small)
        own_rows = w_mid_copy.shape[1]
        block = min(128, own_rows)
        outs = (
            shape(own_rows, hidden),
            shape(own_rows, hidden),
            shape(own_rows, hidden, dtype=BF16),
        )
        new_mom_mid, new_w_mid, mid_copy = call(
            lambda *refs: middle_update(block, paired, *refs),
            outs,
            [VMEM_SPEC] * (3 + len(gradients)),
            "middle_update",
            square,
            out_specs=[HBM_SPEC] * 3,
            scratch=[pltpu.VMEM(out.shape, out.dtype) for out in outs]
            + [pltpu.SemaphoreType.DMA((3 * (own_rows // block),))],
        )(flags, *gradients, mom_mid[0], w_mid_master[0])
        outs = (
            shape(1),
            shape(count, hidden),
            shape(3, 1, hidden),
            shape(count, hidden),
            shape(3, 1, hidden),
            shape(count, hidden, dtype=BF16),
        )
        value, new_w_in, new_vec, new_mom_in, new_mom_vec, in_copy = call(
            lambda *refs: small_update(paths * cores, *refs),
            outs,
            [HBM_SPEC] + [VMEM_SPEC] * 6,
            "small_update",
            0,
            out_specs=[HBM_SPEC] * 6,
            scratch=[pltpu.SMEM((1,), F32)]
            + [pltpu.VMEM(out.shape, out.dtype) for out in outs[1:]]
            + [pltpu.SemaphoreType.DMA((6,))],
        )(far(new_mom_mid), small, small_other, mom_in[0], w_in_master[0], mom_vec.transpose(1, 0, 2), vectors)
        return (
            value,
            new_w_in[None],
            new_w_mid[None],
            new_vec.transpose(1, 0, 2),
            new_mom_in[None],
            new_mom_mid[None],
            new_mom_vec.transpose(1, 0, 2),
            in_copy[None],
            mid_copy[None],
        )

    return shards


def solution(mesh):
    vectors = P("vol", None, None)
    middle = P("vol", "path", None)
    in_specs = (
        P(None, "path"),
        P(None, "path"),
        P("vol", "path"),
        P(None, "vol", "path"),
        P(),
        vectors,
        middle,
        vectors,
        vectors,
        middle,
        vectors,
        middle,
        vectors,
    )
    out_specs = (P("vol"), vectors, middle, vectors, vectors, middle, vectors, vectors, middle)
    return jax.shard_map(step_of(mesh), mesh=mesh, in_specs=in_specs, out_specs=out_specs, check_vma=False)
```

```python
import jax
import jax.numpy as jnp
from jax import lax
from jax.experimental import pallas as pl
from jax.experimental.pallas import tpu as pltpu
from jax.sharding import PartitionSpec as P

MOMENTUM = 0.9
STEP_SIZE = 0.01
LOWER_LEVELS = 4
CORE_SHIFTS = ((4, 2), (1, 3))
SMALL_ROWS = 24
LANES = 128
VMEM_LIMIT = 30 * 1024 * 1024
F32, BF16 = jnp.float32, jnp.bfloat16
VMEM_SPEC = pl.BlockSpec(memory_space=pltpu.VMEM)
HBM_SPEC = pl.BlockSpec(memory_space=pltpu.HBM)


def far(value):
    return pltpu.with_memory_space_constraint(value, pltpu.HBM)


def shape(*dims, dtype=F32):
    return jax.ShapeDtypeStruct(dims, dtype)


def call(kernel, out_shape, in_specs, name, flops, out_specs=None, scratch=()):
    return pl.pallas_call(
        kernel,
        out_shape=out_shape,
        in_specs=in_specs,
        out_specs=out_specs or [VMEM_SPEC] * len(out_shape),
        scratch_shapes=list(scratch),
        compiler_params=pltpu.CompilerParams(vmem_limit_bytes=VMEM_LIMIT),
        cost_estimate=pl.CostEstimate(flops=flops, bytes_accessed=1 << 20, transcendentals=0),
        name=name,
    )


def half_columns(flip, half, width):
    return pl.ds(pl.multiple_of((flip ^ half) * width, width), width)


def is_active(flags):
    return flags[0, 0] > 0.5


def fetch(
    terminal, decisions, ranges, payoff, factors, w_in, vectors,
    rows, payoff_out, factors_out, w_in_out, vectors_out, flags,
    terminal_here, decisions_here, ranges_here, sems,
):
    copies = [
        pltpu.make_async_copy(source, target, sems.at[index])
        for index, (source, target) in enumerate(
            (
                (ranges, ranges_here),
                (terminal, terminal_here),
                (decisions, decisions_here),
                (payoff, payoff_out),
                (factors, factors_out),
                (w_in, w_in_out),
                (vectors, vectors_out),
            )
        )
    ]
    for copy in copies:
        copy.start()
    for copy in copies[:3]:
        copy.wait()
    level = lax.axis_index("vol")
    dates = payoff.shape[0]
    rows[0:1, :] = terminal_here[...]
    for date in range(dates):
        low, high = ranges_here[0, date], ranges_here[1, date]
        inside = jnp.where(jnp.logical_and(level >= low, level <= high), 1.0, 0.0)
        above = jnp.where(level > high, 1.0, 0.0)
        if date == 0:
            flags[0:1, :] = jnp.full((1, LANES), inside)
            flags[1:2, :] = jnp.full((1, LANES), above)
        else:
            rows[dates - date : dates - date + 1, :] = inside * decisions_here[date - 1].astype(F32) + above
    for copy in copies[3:]:
        copy.wait()


def silu_parts(half):
    bent = jnp.tanh(half)
    upper = 1.0 + bent
    act = half * upper
    return act, upper + act * (1.0 - bent)


def first_layer(flip_of, flags, rows, factors, w_in, vectors, rows_out, hidden_one, slope_one):
    rows_out[...] = rows[...]

    @pl.when(is_active(flags))
    def _():
        flip = flip_of()
        hidden = w_in.shape[1]
        width, paths, tile, rows = hidden // 2, factors.shape[1], 256, 16
        for half in range(2):
            columns = half_columns(flip, half, width)
            weights = (0.5 * w_in[:, columns].astype(F32)).astype(BF16)
            bias = 0.5 * vectors[0, :, columns]
            place = slice(half * width, (half + 1) * width)
            for start in range(0, paths, tile):
                pre = lax.dot_general(
                    factors[:, start : start + tile],
                    weights,
                    (((0,), (0,)), ((), ())),
                    preferred_element_type=F32,
                )
                for row in range(0, tile, rows):
                    half_pre = pre[row : row + rows] + bias
                    bent = jnp.tanh(half_pre)
                    squash = 0.5 + 0.5 * bent
                    half_act = half_pre * squash
                    here = slice(start + row, start + row + rows)
                    hidden_one[here, place] = half_act.astype(BF16)
                    slope_one[here, place] = squash + half_act * (1.0 - bent)


def continuation(level, payoff, row_sets):
    dates = payoff.shape[0]
    conts = [jnp.where(level >= below, rows[0:1, :], 0.0) for below, rows in enumerate(row_sets)]
    for date in range(dates - 1, 0, -1):
        updated = []
        for below in range(len(conts) - 1):
            taken = row_sets[below][dates - date : dates - date + 1, :]
            value = taken * (payoff[date : date + 1, :] + conts[below + 1]) + (1.0 - taken) * conts[below]
            updated.append(jnp.where(level >= below, value, 0.0))
        conts = updated
    return conts


def crossing_rows(first, second, after, out):
    del after
    start = 0
    for value in (first, second):
        count = value.shape[0] // 2
        out[start : start + count, :] = value[count:, :]
        start += count


def second_forward(flags, hidden_one, w_own, w_other, vectors, weighted, act_two, partial, joined):
    @pl.when(is_active(flags))
    def _():
        paths, hidden = hidden_one.shape
        width, rows = hidden // 2, 8
        bias, head = 0.5 * vectors[1], vectors[2]
        half_head = 0.5 * head
        joined[:width, :] = w_own[...]
        joined[width:, :] = w_other[...]
        pre = jnp.dot(hidden_one[...], joined[...], preferred_element_type=F32)
        for row in range(0, paths, rows):
            here = slice(row, row + rows)
            act, slope = silu_parts(pre[here] + bias)
            weighted[here, :] = slope * half_head
            act_two[here, :] = act
            terms = act * head
            part = terms[:, :LANES]
            for lane in range(LANES, hidden, LANES):
                part += terms[:, lane : lane + LANES]
            partial[here, :] = part


def exercise_chance(flags, partial, after, chance, parts):
    del after

    @pl.when(is_active(flags))
    def _():
        paths, rows = partial.shape[0], 16
        for row in range(0, paths, rows):
            here = slice(row, row + rows)
            part = partial[here, :]
            upper = part.astype(BF16)
            parts[here, :LANES] = upper
            parts[here, LANES:] = (part - upper.astype(F32)).astype(BF16)
        ones = jnp.ones((2 * LANES, LANES), BF16)
        logits = jnp.dot(parts[...], ones, preferred_element_type=F32)
        chance[...] = 0.5 + 0.5 * jnp.tanh(0.5 * logits)


def second_gradients(sets_of, flags, hidden_one, weighted, act_two, chances, payoff, *refs):
    *row_refs, d_two, grad_other, sums, gains = refs
    level = lax.axis_index("vol")
    paths, hidden = hidden_one.shape
    width, rows = hidden // 2, 16
    lane_tiles = hidden // LANES
    cont_here, cont_below = continuation(level, payoff, sets_of(row_refs))
    gain = payoff[0:1, :] + cont_below - cont_here
    base_value = flags[1, 0] * jnp.sum(gain) + jnp.sum(cont_here)

    @pl.when(jnp.logical_not(is_active(flags)))
    def _():
        grad_other[...] = jnp.zeros(grad_other.shape, BF16)
        sums[...] = jnp.zeros(sums.shape, F32)
        sums[2:3, :] = jnp.full((1, hidden), base_value, F32)

    @pl.when(is_active(flags))
    def _():
        gains[...] = jnp.transpose(jnp.broadcast_to(gain, (LANES, paths)))
        bias_sums = [jnp.zeros((8, LANES), F32) for _ in range(lane_tiles)]
        head_sums = [jnp.zeros((8, LANES), F32) for _ in range(lane_tiles)]
        value_sum = jnp.zeros((rows, LANES), F32)
        for row in range(0, paths, rows):
            here = slice(row, row + rows)
            chance = chances[here, :]
            weight = gains[here, :] * chance
            value_sum += weight
            d_logit = weight * (chance - 1.0)
            for lane in range(lane_tiles):
                place = slice(lane * LANES, (lane + 1) * LANES)
                d_pre = d_logit * weighted[here, place]
                scaled = d_logit * act_two[here, place]
                d_two[here, place] = d_pre.astype(BF16)
                for part in range(0, rows, 8):
                    bias_sums[lane] += d_pre[part : part + 8]
                    head_sums[lane] += scaled[part : part + 8]
        grad_other[...] = lax.dot_general(
            hidden_one[:, width:], d_two[...], (((0,), (0,)), ((), ())), preferred_element_type=F32
        ).astype(BF16)
        value_total = base_value + jnp.sum(value_sum) / LANES
        for lane in range(lane_tiles):
            place = slice(lane * LANES, (lane + 1) * LANES)
            sums[0:1, place] = jnp.sum(bias_sums[lane], axis=0, keepdims=True)
            sums[1:2, place] = jnp.sum(head_sums[lane], axis=0, keepdims=True)
        sums[2:3, :] = jnp.full((1, hidden), value_total, F32)
        sums[3:8, :] = jnp.zeros((5, hidden), F32)


def first_gradients(flip_of, flags, d_two, w_own, w_other, slope_one, factors, sums, small, d_one):
    count = factors.shape[0]
    hidden = d_two.shape[1]
    small[0 : count + 1, :] = jnp.zeros((count + 1, hidden), F32)
    small[count + 1 : count + 4, :] = sums[0:3, :]
    small[count + 4 : SMALL_ROWS, :] = jnp.zeros((SMALL_ROWS - count - 4, hidden), F32)

    @pl.when(is_active(flags))
    def _():
        flip = flip_of()
        paths = d_two.shape[0]
        width, tile, rows = hidden // 2, 512, 16
        for half, weights in enumerate((w_own, w_other)):
            place = slice(half * width, (half + 1) * width)
            bias_sum = jnp.zeros((8, width), F32)
            for start in range(0, paths, tile):
                d_hidden = lax.dot_general(
                    d_two[start : start + tile, :],
                    weights[...],
                    (((1,), (1,)), ((), ())),
                    preferred_element_type=F32,
                )
                for row in range(0, tile, rows):
                    here = slice(start + row, start + row + rows)
                    d_pre = d_hidden[row : row + rows] * slope_one[here, place]
                    d_one[here, place] = d_pre.astype(BF16)
                    for part in range(0, rows, 8):
                        bias_sum += d_pre[part : part + 8]
            columns = half_columns(flip, half, width)
            small[0:count, columns] = jnp.dot(factors[...], d_one[:, place], preferred_element_type=F32)
            small[count : count + 1, columns] = jnp.sum(bias_sum, axis=0, keepdims=True)


def own_gradient(hidden_one, d_two, columns):
    return lax.dot_general(
        hidden_one[:, columns], d_two[...], (((0,), (0,)), ((), ())), preferred_element_type=F32
    )


def plain_gradient(flags, hidden_one, d_two, grad_own):
    grad_own[...] = jnp.zeros(grad_own.shape, BF16)

    @pl.when(is_active(flags))
    def _():
        grad_own[...] = own_gradient(hidden_one, d_two, slice(0, grad_own.shape[0])).astype(BF16)


class Sends:
    def __init__(self, sems):
        self.sems, self.copies = sems, []

    def __call__(self, source, target):
        copy = pltpu.make_async_copy(source, target, self.sems.at[len(self.copies)])
        copy.start()
        self.copies.append(copy)

    def finish(self):
        for copy in self.copies:
            copy.wait()


def middle_update(block, paired, flags, *refs):
    if paired:
        hidden_one, d_two, *refs = refs
    grad, mom_mid, w_mid, new_mom, new_w, new_copy, mom_here, w_here, copy_here, sems = refs

    def write(gradient_of):
        sends = Sends(sems)
        for start in range(0, mom_mid.shape[0], block):
            here = pl.ds(start, block)
            momentum = MOMENTUM * mom_mid[here, :] + 2.0 * gradient_of(start, here)
            mom_here[here, :] = momentum
            master = w_mid[here, :] - STEP_SIZE * momentum
            w_here[here, :] = master
            copy_here[here, :] = master.astype(BF16)
            sends(mom_here.at[here], new_mom.at[here])
            sends(w_here.at[here], new_w.at[here])
            sends(copy_here.at[here], new_copy.at[here])
        sends.finish()

    if not paired:
        write(lambda start, here: grad[here, :].astype(F32))
        return

    @pl.when(is_active(flags))
    def _():
        write(
            lambda start, here: own_gradient(hidden_one, d_two, slice(start, start + block))
            + grad[here, :].astype(F32)
        )

    @pl.when(jnp.logical_not(is_active(flags)))
    def _():
        write(lambda start, here: grad[here, :].astype(F32))


def small_update(
    paths_total, after, small_own, small_other, mom_in, w_in, mom_vec, vec,
    value, new_w_in, new_vec, new_mom_in, new_mom_vec, new_copy,
    value_here, w_in_here, vec_here, mom_in_here, mom_vec_here, copy_here, sems,
):
    del after
    sends = Sends(sems)
    small = small_own[...] + small_other[...]
    count = mom_in.shape[0]
    mom_first = MOMENTUM * mom_in[...] + small[:count]
    first = w_in[...] - STEP_SIZE * mom_first
    mom_in_here[...] = mom_first
    w_in_here[...] = first
    copy_here[...] = first.astype(BF16)
    for row in range(3):
        mom_row = MOMENTUM * mom_vec[row] + small[count + row : count + row + 1]
        mom_vec_here[row] = mom_row
        vec_here[row] = vec[row] - STEP_SIZE * mom_row
    sends(mom_in_here, new_mom_in)
    sends(w_in_here, new_w_in)
    sends(copy_here, new_copy)
    sends(mom_vec_here, new_mom_vec)
    sends(vec_here, new_vec)
    value_here[0] = small[count + 3, 0] / paths_total
    sends(value_here, value)
    sends.finish()


def step_of(mesh):
    levels, cores = mesh.shape["vol"], mesh.shape["path"]
    paired = cores == 2

    def flip_of():
        return lax.axis_index("path") if paired else 0

    def swap(value):
        return lax.ppermute(value, "path", [(0, 1), (1, 0)])

    def shards(
        factors, payoff, terminal, decisions, level_range, w_in_master, w_mid_master, vec_master,
        w_in_copy, w_mid_copy, mom_in, mom_mid, mom_vec,
    ):
        dates, paths = payoff.shape
        count, hidden = w_in_copy.shape[1:]
        width = hidden // 2
        square = 2 * paths * hidden * hidden
        if paired:
            w_own = w_mid_copy[0]
            w_other = swap(w_own)
        else:
            w_full = lax.all_gather(w_mid_copy[0], "path", axis=0, tiled=True)
            w_own, w_other = w_full[:width], w_full[width:]
        vec_hbm = vec_master.transpose(1, 0, 2)
        rows, payoff_near, factors_near, w_in_near, vectors, flags = call(
            fetch,
            (
                shape(dates, paths),
                shape(dates, paths),
                shape(count, paths, dtype=BF16),
                shape(count, hidden, dtype=BF16),
                shape(3, 1, hidden),
                shape(8, LANES),
            ),
            [HBM_SPEC] * 7,
            "fetch",
            0,
            scratch=(
                pltpu.VMEM((1, paths), F32),
                pltpu.VMEM((dates - 1, 1, paths), jnp.int32),
                pltpu.SMEM((2, dates), jnp.int32),
                pltpu.SemaphoreType.DMA((7,)),
            ),
        )(*(far(value) for value in (terminal, decisions, level_range.T, payoff, factors, w_in_copy[0], vec_hbm)))

        rows_after, hidden_one, slope_one = call(
            lambda *refs: first_layer(flip_of, *refs),
            (shape(dates, paths), shape(paths, hidden, dtype=BF16), shape(paths, hidden)),
            [VMEM_SPEC] * 5,
            "first_layer",
            square,
        )(flags, rows, factors_near, w_in_near, vectors)
        if paired:
            both = jnp.concatenate([rows_after, swap(rows)])
            lower = [
                lax.ppermute(
                    both,
                    ("vol", "path"),
                    [
                        (here * 2 + core, (here + below[core]) % levels * 2 + core)
                        for here in range(levels)
                        for core in range(2)
                    ],
                )
                for below in CORE_SHIFTS
            ]
        else:
            row_arrays = (rows,) + tuple(
                lax.ppermute(rows, "vol", [(here, (here + below) % levels) for here in range(levels)])
                for below in range(1, LOWER_LEVELS + 1)
            )

        def sets_of(refs):
            if not paired:
                return [ref[...] for ref in refs]
            own, *lower, crossing = (ref[...] for ref in refs)
            even = lax.axis_index("path") == 0
            sets, start = {0: own}, 0
            for (low, high), value in zip(CORE_SHIFTS, lower):
                size = value.shape[0] // 2
                direct, crossed = value[:size], crossing[start : start + size]
                sets[low] = jnp.where(even, direct, crossed)
                sets[high] = jnp.where(even, crossed, direct)
                start += size
            return [sets[below] for below in range(LOWER_LEVELS + 1)]

        weighted, act_two, partial = call(
            second_forward,
            (shape(paths, hidden), shape(paths, hidden), shape(paths, LANES)),
            [VMEM_SPEC] * 5,
            "second_forward",
            square,
            scratch=(pltpu.VMEM((hidden, hidden), BF16),),
        )(flags, hidden_one, w_own, w_other, vectors)
        after = partial
        if paired:
            crossed = sum(value.shape[0] for value in lower) // 2
            (after,) = call(
                crossing_rows, (shape(crossed, paths),), [VMEM_SPEC] * 3, "crossing_rows", 0
            )(*lower, partial)
            row_arrays = (rows, *lower, swap(after))
        (chances,) = call(
            exercise_chance,
            (shape(paths, LANES),),
            [VMEM_SPEC] * 3,
            "exercise_chance",
            square,
            scratch=(pltpu.VMEM((paths, 2 * LANES), BF16),),
        )(flags, partial, after)
        d_two, grad_other, sums = call(
            lambda *refs: second_gradients(sets_of, *refs),
            (
                shape(paths, hidden, dtype=BF16),
                shape(width, hidden, dtype=BF16),
                shape(8, hidden),
            ),
            [VMEM_SPEC] * (6 + len(row_arrays)),
            "second_gradients",
            square,
            scratch=(pltpu.VMEM((paths, LANES), F32),),
        )(flags, hidden_one, weighted, act_two, chances, payoff_near, *row_arrays)
        if paired:
            grad_other = swap(grad_other)
        (small,) = call(
            lambda *refs: first_gradients(flip_of, *refs),
            (shape(SMALL_ROWS, hidden),),
            [VMEM_SPEC] * 7,
            "first_gradients",
            square,
            scratch=(pltpu.VMEM((paths, hidden), BF16),),
        )(flags, d_two, w_own, w_other, slope_one, factors_near, sums)
        if paired:
            small_other = swap(small)
            gradients = (hidden_one, d_two, grad_other)
        else:
            (grad_own,) = call(
                plain_gradient,
                (shape(width, hidden, dtype=BF16),),
                [VMEM_SPEC] * 3,
                "plain_gradient",
                square,
            )(flags, hidden_one, d_two)
            grads = jnp.concatenate([grad_own, grad_other])
            gradients = (lax.psum_scatter(grads, "path", scatter_dimension=0, tiled=True),)
            small = lax.psum(small, "path")
            small_other = jnp.zeros_like(small)
        own_rows = w_mid_copy.shape[1]
        block = min(128, own_rows)
        outs = (
            shape(own_rows, hidden),
            shape(own_rows, hidden),
            shape(own_rows, hidden, dtype=BF16),
        )
        new_mom_mid, new_w_mid, mid_copy = call(
            lambda *refs: middle_update(block, paired, *refs),
            outs,
            [VMEM_SPEC] * (3 + len(gradients)),
            "middle_update",
            square,
            out_specs=[HBM_SPEC] * 3,
            scratch=[pltpu.VMEM(out.shape, out.dtype) for out in outs]
            + [pltpu.SemaphoreType.DMA((3 * (own_rows // block),))],
        )(flags, *gradients, mom_mid[0], w_mid_master[0])
        outs = (
            shape(1),
            shape(count, hidden),
            shape(3, 1, hidden),
            shape(count, hidden),
            shape(3, 1, hidden),
            shape(count, hidden, dtype=BF16),
        )
        value, new_w_in, new_vec, new_mom_in, new_mom_vec, in_copy = call(
            lambda *refs: small_update(paths * cores, *refs),
            outs,
            [HBM_SPEC] + [VMEM_SPEC] * 6,
            "small_update",
            0,
            out_specs=[HBM_SPEC] * 6,
            scratch=[pltpu.SMEM((1,), F32)]
            + [pltpu.VMEM(out.shape, out.dtype) for out in outs[1:]]
            + [pltpu.SemaphoreType.DMA((6,))],
        )(far(new_mom_mid), small, small_other, mom_in[0], w_in_master[0], mom_vec.transpose(1, 0, 2), vectors)
        return (
            value,
            new_w_in[None],
            new_w_mid[None],
            new_vec.transpose(1, 0, 2),
            new_mom_in[None],
            new_mom_mid[None],
            new_mom_vec.transpose(1, 0, 2),
            in_copy[None],
            mid_copy[None],
        )

    return shards


def solution(mesh):
    vectors = P("vol", None, None)
    middle = P("vol", "path", None)
    in_specs = (
        P(None, "path"),
        P(None, "path"),
        P("vol", "path"),
        P(None, "vol", "path"),
        P(),
        vectors,
        middle,
        vectors,
        vectors,
        middle,
        vectors,
        middle,
        vectors,
    )
    out_specs = (P("vol"), vectors, middle, vectors, vectors, middle, vectors, vectors, middle)
    return jax.shard_map(step_of(mesh), mesh=mesh, in_specs=in_specs, out_specs=out_specs, check_vma=False)
```
